512 devices in a mesh: dp: 32 (over z, y_lo, core), tensor: 16 (over y_hi, x).
Axes of the slice: x: 4, y: 8 (y_hi: 4, y_lo: 2; y = y_hi * 2 + y_lo), z: 8, core: 2. Of those that a mesh axis runs over, the one named last changes fastest.
Arguments:
- decoder_query: bfloat16 [4096, 8192], P('dp', 'tensor'), may hold values from -9 to 9
- decoder_memory: bfloat16 [2, 4096, 8192], P(None, 'dp', 'tensor'), may hold values from -6 to 6
- neighbour_query: bfloat16 [16384, 8192], P(('dp', 'tensor')), may hold values from -9 to 9
- neighbour_key: bfloat16 [16384, 8192], P(('dp', 'tensor')), may hold values from -6 to 6
- neighbour_value: bfloat16 [16384, 8192], P(('dp', 'tensor')), may hold values from -6 to 6
- neighbour_table: int32 [64, 2], P('dp'), may hold values from 0 to 3, as said below
- output_weight: bfloat16 [8192, 8192], P('tensor', 'dp'), may hold values from -1 to 1
Outputs:
- layer_output: bfloat16 [4096, 8192], P('dp', 'tensor')
The draws below stay inside these ranges and needn't reach their ends.
Inputs may be any that keep to these rules, and one draw needn't show every extreme that they name: `neighbour_table`: within the 4 entries of each index of dp (its 2 stretches), every number 0 to 3 appears exactly once.
All inputs are finite; a program needn't handle non-finite values.
Results may differ from the reference program's by a relative error of at most 0.018.
Values may be sent and summed in bfloat16 or wider, within the bound.
No kernel may reach another device: no remote copies, remote signals or barrier semaphores. Data moves between devices by JAX's collectives and lax.ppermute only.
A program may use at most 64 MiB of HBM per device.

```python
import math
import jax
import jax.numpy as jnp
from jax import lax

D = 8192
HEADS = 64
HD = 128
STRETCH = 64
NEIGH = 2
NBLEN = 128
TOK_DEV = 128
TOKENS = 4096
STRETCHES = 64
NB_DEV = 4
NBTOK = 16384
HC = 8192
N_TENSOR = 16


def base_normal(key, row_count):
    return jnp.clip(jax.random.normal(key, (row_count, HEADS * HD), jnp.float32), -6.0, 6.0)


def draw_decoder_query(key, part):
    key = jax.random.fold_in(key, 3)
    values = base_normal(key, TOKENS)
    return values.astype(jnp.bfloat16)


def draw_decoder_memory(key, part):
    key = jax.random.fold_in(key, 7)
    keys_part = base_normal(jax.random.fold_in(key, 1), TOKENS)
    values_part = base_normal(jax.random.fold_in(key, 2), TOKENS)
    return jnp.stack([keys_part, values_part]).astype(jnp.bfloat16)


def draw_neighbour_query(key, part):
    key = jax.random.fold_in(key, 13)
    values = base_normal(key, NBTOK)
    return values.astype(jnp.bfloat16)


def draw_neighbour_key(key, part):
    key = jax.random.fold_in(key, 17)
    values = base_normal(key, NBTOK)
    return values.astype(jnp.bfloat16)


def draw_neighbour_table(key, part):
    key = jax.random.fold_in(key, 19)
    group_count = TOKENS // TOK_DEV
    group_keys = jax.random.split(key, group_count)
    orders = jax.vmap(lambda single: jax.random.permutation(single, NB_DEV))(group_keys)
    return orders.reshape(STRETCHES, NEIGH).astype(jnp.int32)


def with_spikes(entries, own_key, source, target, blocks, factor):
    def block_of(position):
        return (jnp.arange(entries.shape[position]) // (entries.shape[position] // blocks)).reshape((-1,) + (1,) * (entries.ndim - 1 - position))

    first = jax.random.permutation(own_key, blocks)[block_of(target)]
    other_side = (block_of(target) + blocks // 2) % blocks
    return jnp.where((block_of(source) == first) | (block_of(source) == other_side), factor * entries, entries)


def level_of(key, extent, pieces, smallest, largest):
    loudness, own = 1.0, jax.random.fold_in(key, 6)
    for position, parts in pieces:
        draws = jnp.exp(jax.random.uniform(jax.random.fold_in(own, position), (parts,), jnp.float32, smallest / len(pieces), largest / len(pieces)))
        loudness = loudness * jnp.repeat(draws, extent[position] // parts).reshape([-1 if axis == position else 1 for axis in range(len(extent))])
    return loudness


def gaussian(key, shape, scale, reach, pieces=(), kind=jnp.bfloat16):
    result = scale * jax.random.normal(key, shape, jnp.float32)
    if pieces:
        result = result * level_of(key, shape, pieces, -0.22, 0.18)
    return jnp.clip(result, -reach, reach).astype(kind)


def noise_with(rng, shape, deviation, bound, pieces, heavy, kind=jnp.bfloat16):
    result = deviation * jax.random.normal(rng, shape, jnp.float32)
    if pieces:
        result = result * level_of(rng, shape, pieces, -0.22, 0.18)
    return jnp.clip(with_spikes(result, jax.random.fold_in(rng, 3), *heavy), -bound, bound).astype(kind)


def setup_inputs(seed: int = 0) -> dict:
    key_list = jax.random.split(jax.random.key(seed), 8)
    decoder_query = draw_decoder_query(jax.random.fold_in(key_list[7], 71), 0)
    decoder_memory = draw_decoder_memory(jax.random.fold_in(key_list[7], 71), 0)
    neighbour_query = draw_neighbour_query(jax.random.fold_in(key_list[7], 71), 0)
    neighbour_key = draw_neighbour_key(jax.random.fold_in(key_list[7], 71), 0)
    neighbour_value = gaussian(key_list[4], (NBTOK, HC), 1.0, 6.0, ((0, 512),))
    neighbour_table = draw_neighbour_table(jax.random.fold_in(key_list[7], 71), 0)
    output_weight = noise_with(key_list[6], (HC, D), HD ** -0.5, 1.0, ((0, 16), (1, 32)), (0, 1, 32, 2.75))
    return dict(decoder_query=decoder_query, decoder_memory=decoder_memory, neighbour_query=neighbour_query, neighbour_key=neighbour_key, neighbour_value=neighbour_value, neighbour_table=neighbour_table, output_weight=output_weight)


def softmax_rows(scores):
    row_top = lax.optimization_barrier(jnp.max(scores, axis=-1, keepdims=True))
    expo = jnp.exp(scores - row_top)
    return expo / lax.optimization_barrier(jnp.sum(expo, axis=-1, keepdims=True))

def rounded(values):
    return lax.optimization_barrier(values.astype(jnp.bfloat16)).astype(jnp.float32)

def reference(decoder_query, decoder_memory, neighbour_query, neighbour_key, neighbour_value, neighbour_table, output_weight):
    score_scale = 1.0 / math.sqrt(HD)
    per_group = TOK_DEV // STRETCH
    total_nbrs = STRETCHES * NEIGH
    offsets = jnp.arange(STRETCHES, dtype=jnp.int32) // per_group * NB_DEV
    global_table = (neighbour_table + offsets[:, None]).astype(jnp.int32)
    flat_table = global_table.reshape(-1)
    slot_stretch = jnp.arange(total_nbrs, dtype=jnp.int32) // NEIGH
    matches = (flat_table[None, :] == jnp.arange(total_nbrs, dtype=jnp.int32)[:, None]).astype(jnp.int32)
    stretch_of = lax.optimization_barrier(jnp.sum(matches * slot_stretch[None, :], axis=1)).astype(jnp.int32)
    stretch_keys = decoder_memory[0].reshape(STRETCHES, STRETCH, HEADS, HD)
    stretch_values = decoder_memory[1].reshape(STRETCHES, STRETCH, HEADS, HD)
    nbr_queries = neighbour_query.reshape(total_nbrs, NBLEN, HEADS, HD)
    nbr_values = neighbour_value.reshape(total_nbrs, NBLEN, HC)

    def encode(nbr_index):
        owner = stretch_of[nbr_index]
        query_block = nbr_queries[nbr_index].astype(jnp.float32)
        key_block = stretch_keys[owner].astype(jnp.float32)
        value_block = stretch_values[owner].astype(jnp.float32)
        scores = jnp.einsum('rhd,chd->hrc', query_block, key_block) * score_scale
        probs = rounded(softmax_rows(scores))
        context = jnp.einsum('hrc,chd->rhd', probs, value_block).reshape(NBLEN, HC)
        return (nbr_values[nbr_index].astype(jnp.float32) + context).astype(jnp.bfloat16)
    encoded = lax.map(encode, jnp.arange(total_nbrs, dtype=jnp.int32))
    token_queries = decoder_query.reshape(STRETCHES, STRETCH, HEADS, HD)
    nbr_keys = neighbour_key.reshape(total_nbrs, NBLEN, HEADS, HD)
    encoded_heads = encoded.reshape(total_nbrs, NBLEN, HEADS, HD)

    def decode(stretch_index):
        chosen = global_table[stretch_index]
        key_block = nbr_keys[chosen].reshape(NEIGH * NBLEN, HEADS, HD).astype(jnp.float32)
        value_block = encoded_heads[chosen].reshape(NEIGH * NBLEN, HEADS, HD).astype(jnp.float32)
        query_block = token_queries[stretch_index].astype(jnp.float32)
        scores = jnp.einsum('thd,khd->htk', query_block, key_block) * score_scale
        probs = rounded(softmax_rows(scores))
        context = jnp.einsum('htk,khd->thd', probs, value_block)
        return context.reshape(STRETCH, HC).astype(jnp.bfloat16)
    context_all = lax.map(decode, jnp.arange(STRETCHES, dtype=jnp.int32)).reshape(TOKENS, HC)
    group_cols = HC // N_TENSOR

    def add_group(total, group_index):
        start_col = (group_index * group_cols).astype(jnp.int32)
        columns = lax.dynamic_slice_in_dim(context_all, start_col, group_cols, 1)
        weight_rows = lax.dynamic_slice_in_dim(output_weight, start_col, group_cols, 0)
        partial_value = jnp.dot(columns, weight_rows, preferred_element_type=jnp.float32)
        return (total + rounded(partial_value), None)
    total, _ = lax.scan(add_group, jnp.zeros((TOKENS, D), jnp.float32), jnp.arange(N_TENSOR, dtype=jnp.int32))
    return total.astype(jnp.bfloat16)
```

```python
import functools
import math

import jax
import jax.numpy as jnp
from jax import lax
from jax.experimental import pallas as pl
from jax.experimental.pallas import tpu as pltpu
from jax.sharding import Mesh
from jax.sharding import PartitionSpec as P

HD = 128
STRETCH = 64
NBLEN = 128
SCALE = 1.0 / math.sqrt(HD)

AXES = ("z", "yl", "c", "yh", "x")
DP = ("z", "yl", "c")
TENSOR = ("yh", "x")


def softmax_rows(scores):
    row_top = jnp.max(scores, axis=-1, keepdims=True)
    expo = jnp.exp(scores - row_top)
    return (expo / jnp.sum(expo, axis=-1, keepdims=True)).astype(jnp.bfloat16)


def rows_times_rows(left, right):
    return lax.dot_general(
        left, right, (((1,), (1,)), ((), ())), preferred_element_type=jnp.float32
    )


def attention_kernel(table_ref, query_ref, memory_ref, qv_ref, key_ref, out_ref):
    stretches, per_stretch = table_ref.shape
    pieces = key_ref.shape[0] // (stretches * per_stretch)
    heads = query_ref.shape[1] // HD
    for u in range(stretches):
        rows = slice(u * STRETCH, (u + 1) * STRETCH)
        for h in range(heads):
            cols = slice(h * HD, (h + 1) * HD)
            mem_key = memory_ref[0, rows, cols]
            mem_value = memory_ref[1, rows, cols]
            query = query_ref[rows, cols]
            nbr_query, nbr_value, nbr_key = [], [], []
            for j in range(per_stretch):
                here = pl.ds(table_ref[u, j] * pieces, pieces)
                nbr_query.append(qv_ref[here, 0, :, cols].reshape(NBLEN, HD))
                nbr_value.append(qv_ref[here, 1, :, cols].reshape(NBLEN, HD))
                nbr_key.append(key_ref[here, :, cols].reshape(NBLEN, HD))
            nbr_query = jnp.concatenate(nbr_query, axis=0)
            nbr_value = jnp.concatenate(nbr_value, axis=0)
            nbr_key = jnp.concatenate(nbr_key, axis=0)
            enc_probs = softmax_rows(rows_times_rows(nbr_query, mem_key) * SCALE)
            encoded = nbr_value.astype(jnp.float32) + jnp.dot(
                enc_probs, mem_value, preferred_element_type=jnp.float32
            )
            encoded = encoded.astype(jnp.bfloat16)
            dec_probs = softmax_rows(rows_times_rows(query, nbr_key) * SCALE)
            context = jnp.dot(dec_probs, encoded, preferred_element_type=jnp.float32)
            out_ref[rows, cols] = context.astype(jnp.bfloat16)


def attention(table, query, memory, qv, key):
    vmem = pl.BlockSpec(memory_space=pltpu.VMEM)
    return pl.pallas_call(
        attention_kernel,
        out_shape=jax.ShapeDtypeStruct(query.shape, jnp.bfloat16),
        in_specs=[pl.BlockSpec(memory_space=pltpu.SMEM)] + [vmem] * 4,
        out_specs=vmem,
        compiler_params=pltpu.CompilerParams(vmem_limit_bytes=24 * 2**20),
    )(table, query, memory, qv, key)


def project_kernel(context_ref, weight_ref, out_ref, total):
    step = pl.program_id(0)

    @pl.when(step == 0)
    def _():
        total[...] = jnp.zeros_like(total)

    group = context_ref[0]
    width = weight_ref.shape[-1]
    for part in range(weight_ref.shape[1]):
        cols = slice(part * width, (part + 1) * width)
        total[:, cols] += jnp.dot(
            group, weight_ref[0, part], preferred_element_type=jnp.float32
        )

    @pl.when(step == pl.num_programs(0) - 1)
    def _():
        out_ref[...] = total[...].astype(jnp.bfloat16)


def project(context, weight):
    groups, tokens, span = context.shape
    _, parts, _, width = weight.shape
    return pl.pallas_call(
        project_kernel,
        grid=(groups,),
        out_shape=jax.ShapeDtypeStruct((tokens, parts * width), jnp.bfloat16),
        in_specs=[
            pl.BlockSpec((1, tokens, span), lambda i: (i, 0, 0)),
            pl.BlockSpec((1, parts, span, width), lambda i: (i, 0, 0, 0)),
        ],
        out_specs=pl.BlockSpec((tokens, parts * width), lambda i: (0, 0)),
        scratch_shapes=[pltpu.VMEM((tokens, parts * width), jnp.float32)],
        compiler_params=pltpu.CompilerParams(vmem_limit_bytes=24 * 2**20),
    )(context, weight)


def gather4(value, axis):
    size = 4
    ahead = [(i, (i + 1) % size) for i in range(size)]
    behind = [(i, (i - 1) % size) for i in range(size)]
    from_left = lax.ppermute(value, axis, ahead)
    from_right = lax.ppermute(value, axis, behind)
    half = value.shape[0] // 2
    far_top = lax.ppermute(from_left[:half], axis, ahead)
    far_low = lax.ppermute(from_right[half:], axis, behind)
    return [value, from_left, jnp.concatenate([far_top, far_low], axis=0), from_right]


def local(
    decoder_query,
    decoder_memory,
    neighbour_query,
    neighbour_key,
    neighbour_value,
    neighbour_table,
    output_weight,
    *,
    groups,
):
    swap = [(a * groups + b, b * groups + a) for a in range(groups) for b in range(groups)]
    moved = lax.ppermute(output_weight, ("z", "yl", "yh", "x"), swap)
    weight = lax.all_gather(moved, DP, axis=0, tiled=False)
    weight = weight.reshape(groups, 2, *moved.shape)

    rows, all_cols = neighbour_query.shape
    span = all_cols // groups
    qv = jnp.stack([neighbour_query, neighbour_value]).reshape(2, rows, groups, span)
    qv = lax.all_to_all(
        qv.transpose(2, 0, 1, 3), TENSOR, split_axis=0, concat_axis=0, tiled=True
    )
    key = neighbour_key.reshape(rows, groups, span).transpose(1, 0, 2)
    key = lax.all_to_all(key, TENSOR, split_axis=0, concat_axis=0, tiled=True)

    context = attention(neighbour_table, decoder_query, decoder_memory, qv, key)
    context = lax.all_gather(context, "yh", axis=0, tiled=False)
    tokens = context.shape[1]
    context = context.transpose(1, 0, 2).reshape(tokens, -1)
    pieces = gather4(context, "x")
    here = lax.axis_index("x")
    stacked = jnp.stack(pieces)
    order = (here - jnp.arange(4, dtype=jnp.int32)) % 4
    stacked = stacked[order]
    context = stacked.reshape(4, tokens, 4, span).transpose(2, 0, 1, 3)
    context = context.reshape(groups, tokens, span)
    return project(context, weight)


def solution(mesh):
    groups = mesh.shape["tensor"]
    inner = Mesh(mesh.devices.reshape(8, 2, 2, 4, 4), AXES)
    return jax.shard_map(
        functools.partial(local, groups=groups),
        mesh=inner,
        in_specs=(
            P(DP, TENSOR),
            P(None, DP, TENSOR),
            P(AXES, None),
            P(AXES, None),
            P(AXES, None),
            P(DP, None),
            P(TENSOR, DP),
        ),
        out_specs=P(DP, TENSOR),
        check_vma=False,
    )
```

```python
import functools
import math

import jax
import jax.numpy as jnp
from jax import lax
from jax.experimental import pallas as pl
from jax.experimental.pallas import tpu as pltpu
from jax.sharding import Mesh
from jax.sharding import PartitionSpec as P

HD = 128
STRETCH = 64
NBLEN = 128
SCALE = 1.0 / math.sqrt(HD)

AXES = ("z", "yl", "c", "yh", "x")
DP = ("z", "yl", "c")
TENSOR = ("yh", "x")


def softmax_rows(scores):
    row_top = jnp.max(scores, axis=-1, keepdims=True)
    expo = jnp.exp(scores - row_top)
    return (expo / jnp.sum(expo, axis=-1, keepdims=True)).astype(jnp.bfloat16)


def rows_times_rows(left, right):
    return lax.dot_general(
        left, right, (((1,), (1,)), ((), ())), preferred_element_type=jnp.float32
    )


def attention_kernel(table_ref, query_ref, memory_ref, nbr_ref, out_ref):
    stretches, per_stretch = table_ref.shape
    pieces = nbr_ref.shape[0] // (stretches * per_stretch)
    heads = query_ref.shape[1] // HD
    for u in range(stretches):
        rows = slice(u * STRETCH, (u + 1) * STRETCH)
        places = [pl.ds(table_ref[u, j] * pieces, pieces) for j in range(per_stretch)]
        for h in range(heads):
            cols = slice(h * HD, (h + 1) * HD)
            nbr_query, nbr_key, nbr_value = (
                jnp.concatenate(
                    [nbr_ref[place, kind, :, cols].reshape(NBLEN, HD) for place in places],
                    axis=0,
                )
                for kind in range(3)
            )
            enc_probs = softmax_rows(
                rows_times_rows(nbr_query, memory_ref[0, rows, cols]) * SCALE
            )
            encoded = nbr_value.astype(jnp.float32) + jnp.dot(
                enc_probs, memory_ref[1, rows, cols], preferred_element_type=jnp.float32
            )
            encoded = encoded.astype(jnp.bfloat16)
            dec_probs = softmax_rows(
                rows_times_rows(query_ref[rows, cols], nbr_key) * SCALE
            )
            context = jnp.dot(dec_probs, encoded, preferred_element_type=jnp.float32)
            context = context.astype(jnp.bfloat16)
            for copy in range(out_ref.shape[0]):
                out_ref[copy, rows, cols] = context


VMEM = pl.BlockSpec(memory_space=pltpu.VMEM)
PARAMS = pltpu.CompilerParams(vmem_limit_bytes=32 * 2**20)


def attention(table, query, memory, neighbours, copies):
    return pl.pallas_call(
        attention_kernel,
        out_shape=jax.ShapeDtypeStruct((copies, *query.shape), jnp.bfloat16),
        in_specs=[pl.BlockSpec(memory_space=pltpu.SMEM)] + [VMEM] * 3,
        out_specs=VMEM,
        compiler_params=PARAMS,
    )(table, query, memory, neighbours)


def fold_kernel(weight_ref, out_ref):
    copies, quarters, half, _ = out_ref.shape
    width = weight_ref.shape[1] // quarters
    for q in range(quarters):
        cols = slice(q * width, (q + 1) * width)
        block = jnp.concatenate([weight_ref[:half, cols], weight_ref[half:, cols]], axis=1)
        for copy in range(copies):
            out_ref[copy, q] = block


def fold(weight, copies, quarters):
    rows, cols = weight.shape
    shape = (copies, quarters, rows // 2, 2 * cols // quarters)
    return pl.pallas_call(
        fold_kernel,
        out_shape=jax.ShapeDtypeStruct(shape, weight.dtype),
        in_specs=[VMEM],
        out_specs=VMEM,
        compiler_params=PARAMS,
    )(weight)


def unfold_kernel(folded_ref, out_ref):
    _, quarters, half, width = folded_ref.shape
    middle = width // 2
    for q in range(quarters):
        first, second = folded_ref[0, q], folded_ref[1, q]
        upper = jnp.concatenate([first[:, :middle], second[:, :middle]], axis=1)
        lower = jnp.concatenate([first[:, middle:], second[:, middle:]], axis=1)
        out_ref[pl.ds(2 * q * half, half), :] = upper
        out_ref[pl.ds((2 * q + 1) * half, half), :] = lower


def unfold(folded):
    _, quarters, half, width = folded.shape
    return pl.pallas_call(
        unfold_kernel,
        out_shape=jax.ShapeDtypeStruct((2 * quarters * half, width), folded.dtype),
        in_specs=[VMEM],
        out_specs=VMEM,
        compiler_params=PARAMS,
    )(folded)


def project_kernel(context_ref, weight_ref, out_ref):
    sides, quarters, tokens, span = context_ref.shape
    half = tokens // 2
    total = None
    weight = jnp.concatenate([weight_ref[0], weight_ref[1]], axis=1)
    for q in range(quarters):
        left = jnp.concatenate([context_ref[s, q] for s in range(sides)], axis=0)
        term = jnp.dot(
            left, weight[q * span : (q + 1) * span], preferred_element_type=jnp.float32
        )
        total = term if total is None else total + term
    width = weight_ref.shape[2]
    for s in range(sides):
        upper = total[s * tokens : s * tokens + half].astype(jnp.bfloat16)
        lower = total[s * tokens + half : (s + 1) * tokens].astype(jnp.bfloat16)
        for piece in range(out_ref.shape[1]):
            cols = slice(piece * width // 2, (piece + 1) * width // 2)
            out_ref[s, piece] = jnp.concatenate([upper[:, cols], lower[:, cols]], axis=1)


def project(context, weight):
    sides, quarters, tokens, span = context.shape
    planes, depth, width = weight.shape
    return pl.pallas_call(
        project_kernel,
        grid=(planes // 2,),
        out_shape=jax.ShapeDtypeStruct((sides, 2 * planes, tokens // 2, width), jnp.bfloat16),
        in_specs=[
            pl.BlockSpec(context.shape, lambda i: (0, 0, 0, 0)),
            pl.BlockSpec((2, depth, width), lambda i: (i, 0, 0)),
        ],
        out_specs=pl.BlockSpec((sides, 4, tokens // 2, width), lambda i: (0, i, 0, 0)),
        compiler_params=PARAMS,
    )(context, weight)


def add_kernel(partial_ref, out_ref):
    sides, senders, quarters, half, width = partial_ref.shape
    for s in range(sides):
        for pair in range(quarters // 2):
            sums = []
            for q in (2 * pair, 2 * pair + 1):
                total = partial_ref[s, 0, q].astype(jnp.float32)
                for sender in range(1, senders):
                    total += partial_ref[s, sender, q].astype(jnp.float32)
                sums.append(total.astype(jnp.bfloat16))
            first, second = sums
            middle = width // 2
            cols = pl.ds((s * (quarters // 2) + pair) * width, width)
            out_ref[:half, cols] = jnp.concatenate(
                [first[:, :middle], second[:, :middle]], axis=1
            )
            out_ref[half:, cols] = jnp.concatenate(
                [first[:, middle:], second[:, middle:]], axis=1
            )


def add(partial):
    sides, _, quarters, half, width = partial.shape
    return pl.pallas_call(
        add_kernel,
        out_shape=jax.ShapeDtypeStruct((2 * half, sides * quarters * width // 2), jnp.bfloat16),
        in_specs=[VMEM],
        out_specs=VMEM,
        compiler_params=PARAMS,
    )(partial)


def exchange(value, axes):
    return lax.all_to_all(value, axes, split_axis=0, concat_axis=0, tiled=True)


def local(
    decoder_query,
    decoder_memory,
    neighbour_query,
    neighbour_key,
    neighbour_value,
    neighbour_table,
    output_weight,
    *,
    groups,
):
    folded = fold(output_weight, 2, 4)
    shape = folded.shape
    folded = exchange(folded.reshape(8, *shape[2:]), ("yl", "x")).reshape(shape)
    weight = lax.all_gather(unfold(folded), "z", axis=0, tiled=False)

    rows, all_cols = neighbour_query.shape
    span = all_cols // groups
    neighbours = jnp.stack([neighbour_query, neighbour_key, neighbour_value])
    neighbours = neighbours.reshape(3, rows, groups, span).transpose(2, 0, 1, 3)
    neighbours = exchange(neighbours, TENSOR)

    context = attention(neighbour_table, decoder_query, decoder_memory, neighbours, 8)
    context = exchange(context, ("c", "x"))
    context = context.reshape(2, 4, *context.shape[1:])
    partial = project(context, weight)
    shape = partial.shape
    partial = exchange(partial.reshape(2 * groups, *shape[2:]), ("c", "yh", "x"))
    return add(partial.reshape(2, 4, 4, *shape[2:]))


def solution(mesh):
    groups = mesh.shape["tensor"]
    inner = Mesh(mesh.devices.reshape(8, 2, 2, 4, 4), AXES)
    return jax.shard_map(
        functools.partial(local, groups=groups),
        mesh=inner,
        in_specs=(
            P(DP, TENSOR),
            P(None, DP, TENSOR),
            P(AXES, None),
            P(AXES, None),
            P(AXES, None),
            P(DP, None),
            P(TENSOR, DP),
        ),
        out_specs=P(DP, TENSOR),
        check_vma=False,
    )
```

```python
import functools
import math

import jax
import jax.numpy as jnp
from jax import lax
from jax.experimental import pallas as pl
from jax.experimental.pallas import tpu as pltpu
from jax.sharding import Mesh
from jax.sharding import PartitionSpec as P

HD = 128
STRETCH = 64
NBLEN = 128
SCALE = 1.0 / math.sqrt(HD)

AXES = ("z", "yl", "c", "yh", "x")
DP = ("z", "yl", "c")
TENSOR = ("yh", "x")


def softmax_rows(scores):
    row_top = jnp.max(scores, axis=-1, keepdims=True)
    expo = jnp.exp(scores - row_top)
    return (expo / jnp.sum(expo, axis=-1, keepdims=True)).astype(jnp.bfloat16)


def rows_times_rows(left, right):
    return lax.dot_general(
        left, right, (((1,), (1,)), ((), ())), preferred_element_type=jnp.float32
    )


def attention_kernel(table_ref, query_ref, memory_ref, nbr_ref, out_ref):
    stretches, per_stretch = table_ref.shape
    pieces = nbr_ref.shape[0] // (stretches * per_stretch)
    heads = query_ref.shape[1] // HD
    for u in range(stretches):
        rows = slice(u * STRETCH, (u + 1) * STRETCH)
        places = [pl.ds(table_ref[u, j] * pieces, pieces) for j in range(per_stretch)]
        for h in range(heads):
            cols = slice(h * HD, (h + 1) * HD)
            nbr_query, nbr_key, nbr_value = (
                jnp.concatenate(
                    [nbr_ref[place, kind, :, cols].reshape(NBLEN, HD) for place in places],
                    axis=0,
                )
                for kind in range(3)
            )
            enc_probs = softmax_rows(
                rows_times_rows(nbr_query, memory_ref[0, rows, cols]) * SCALE
            )
            encoded = nbr_value.astype(jnp.float32) + jnp.dot(
                enc_probs, memory_ref[1, rows, cols], preferred_element_type=jnp.float32
            )
            encoded = encoded.astype(jnp.bfloat16)
            dec_probs = softmax_rows(
                rows_times_rows(query_ref[rows, cols], nbr_key) * SCALE
            )
            context = jnp.dot(dec_probs, encoded, preferred_element_type=jnp.float32)
            context = context.astype(jnp.bfloat16)
            for copy in range(out_ref.shape[0]):
                out_ref[copy, rows, cols] = context


VMEM = pl.BlockSpec(memory_space=pltpu.VMEM)
PARAMS = pltpu.CompilerParams(vmem_limit_bytes=32 * 2**20)


def attention(table, query, memory, neighbours, copies):
    return pl.pallas_call(
        attention_kernel,
        out_shape=jax.ShapeDtypeStruct((copies, *query.shape), jnp.bfloat16),
        in_specs=[pl.BlockSpec(memory_space=pltpu.SMEM)] + [VMEM] * 3,
        out_specs=VMEM,
        compiler_params=PARAMS,
    )(table, query, memory, neighbours)


def fold_kernel(weight_ref, out_ref):
    copies, quarters, half, _ = out_ref.shape
    width = weight_ref.shape[1] // quarters
    for q in range(quarters):
        cols = slice(q * width, (q + 1) * width)
        block = jnp.concatenate([weight_ref[:half, cols], weight_ref[half:, cols]], axis=1)
        for copy in range(copies):
            out_ref[copy, q] = block


def fold(weight, copies, quarters):
    rows, cols = weight.shape
    shape = (copies, quarters, rows // 2, 2 * cols // quarters)
    return pl.pallas_call(
        fold_kernel,
        out_shape=jax.ShapeDtypeStruct(shape, weight.dtype),
        in_specs=[VMEM],
        out_specs=VMEM,
        compiler_params=PARAMS,
    )(weight)


def unfold_kernel(folded_ref, out_ref):
    _, quarters, half, width = folded_ref.shape
    middle = width // 2
    for q in range(quarters):
        first, second = folded_ref[0, q], folded_ref[1, q]
        upper = jnp.concatenate([first[:, :middle], second[:, :middle]], axis=1)
        lower = jnp.concatenate([first[:, middle:], second[:, middle:]], axis=1)
        out_ref[pl.ds(2 * q * half, half), :] = upper
        out_ref[pl.ds((2 * q + 1) * half, half), :] = lower


def unfold(folded):
    _, quarters, half, width = folded.shape
    return pl.pallas_call(
        unfold_kernel,
        out_shape=jax.ShapeDtypeStruct((2 * quarters * half, width), folded.dtype),
        in_specs=[VMEM],
        out_specs=VMEM,
        compiler_params=PARAMS,
    )(folded)


def pack_kernel(query_ref, key_ref, value_ref, out_ref):
    groups, _, _, span = out_ref.shape
    for kind, ref in enumerate((query_ref, key_ref, value_ref)):
        for g in range(groups):
            out_ref[g, kind] = ref[:, g * span : (g + 1) * span]


def pack(query, key, value, groups):
    rows, cols = query.shape
    return pl.pallas_call(
        pack_kernel,
        out_shape=jax.ShapeDtypeStruct((groups, 3, rows, cols // groups), query.dtype),
        in_specs=[VMEM] * 3,
        out_specs=VMEM,
        compiler_params=PARAMS,
    )(query, key, value)


def project_kernel(context_ref, weight_ref, out_ref):
    quarters, _, span = context_ref.shape
    _, sides, _, width = weight_ref.shape
    total = None
    for q in range(quarters):
        rows = slice(q * span, (q + 1) * span)
        right = jnp.concatenate([weight_ref[0, s, rows] for s in range(sides)], axis=1)
        term = jnp.dot(context_ref[q], right, preferred_element_type=jnp.float32)
        total = term if total is None else total + term
    total = total.astype(jnp.bfloat16)
    middle = width // 2
    for piece in range(2):
        out_ref[piece] = jnp.concatenate(
            [
                total[:, s * width + piece * middle : s * width + (piece + 1) * middle]
                for s in range(sides)
            ],
            axis=1,
        )


def project(context, weight):
    quarters, tokens, span = context.shape
    planes, sides, depth, width = weight.shape
    return pl.pallas_call(
        project_kernel,
        grid=(planes,),
        out_shape=jax.ShapeDtypeStruct((2 * planes, tokens, width), jnp.bfloat16),
        in_specs=[
            pl.BlockSpec(context.shape, lambda i: (0, 0, 0)),
            pl.BlockSpec((1, sides, depth, width), lambda i: (i, 0, 0, 0)),
        ],
        out_specs=pl.BlockSpec((2, tokens, width), lambda i: (i, 0, 0)),
        compiler_params=pltpu.CompilerParams(vmem_limit_bytes=56 * 2**20),
    )(context, weight)


def add_kernel(partial_ref, out_ref):
    senders, quarters, _, width = partial_ref.shape
    middle = width // 2
    for pair in range(quarters // 2):
        sums = []
        for q in (2 * pair, 2 * pair + 1):
            total = partial_ref[0, q].astype(jnp.float32)
            for sender in range(1, senders):
                total += partial_ref[sender, q].astype(jnp.float32)
            sums.append(total.astype(jnp.bfloat16))
        for s in range(2):
            part = slice(s * middle, (s + 1) * middle)
            cols = pl.ds((s * (quarters // 2) + pair) * width, width)
            out_ref[:, cols] = jnp.concatenate([one[:, part] for one in sums], axis=1)


def add(partial):
    _, quarters, tokens, width = partial.shape
    return pl.pallas_call(
        add_kernel,
        out_shape=jax.ShapeDtypeStruct((tokens, quarters * width), jnp.bfloat16),
        in_specs=[VMEM],
        out_specs=VMEM,
        compiler_params=PARAMS,
    )(partial)


def exchange(value, axes):
    return lax.all_to_all(value, axes, split_axis=0, concat_axis=0, tiled=True)


def local(
    decoder_query,
    decoder_memory,
    neighbour_query,
    neighbour_key,
    neighbour_value,
    neighbour_table,
    output_weight,
    *,
    groups,
):
    folded = fold(output_weight, 2, 4)
    shape = folded.shape
    folded = exchange(folded.reshape(8, *shape[2:]), ("yl", "x")).reshape(shape)
    weight = lax.all_gather(unfold(folded), ("z", "c"), axis=0, tiled=False)
    weight = weight.reshape(8, 2, *weight.shape[1:])

    neighbours = pack(neighbour_query, neighbour_key, neighbour_value, groups)
    neighbours = exchange(neighbours, TENSOR)
    context = attention(neighbour_table, decoder_query, decoder_memory, neighbours, 4)
    context = exchange(context, "x")
    partial = exchange(project(context, weight), TENSOR)
    return add(partial.reshape(4, 4, *partial.shape[1:]))


def solution(mesh):
    groups = mesh.shape["tensor"]
    inner = Mesh(mesh.devices.reshape(8, 2, 2, 4, 4), AXES)
    return jax.shard_map(
        functools.partial(local, groups=groups),
        mesh=inner,
        in_specs=(
            P(DP, TENSOR),
            P(None, DP, TENSOR),
            P(AXES, None),
            P(AXES, None),
            P(AXES, None),
            P(DP, None),
            P(TENSOR, DP),
        ),
        out_specs=P(DP, TENSOR),
        check_vma=False,
    )
```

```python
import functools
import math

import jax
import jax.numpy as jnp
from jax import lax
from jax.experimental import pallas as pl
from jax.experimental.pallas import tpu as pltpu
from jax.sharding import Mesh
from jax.sharding import PartitionSpec as P

HD = 128
STRETCH = 64
NBLEN = 128
SCALE = 1.0 / math.sqrt(HD)

AXES = ("z", "yl", "c", "yh", "x")
DP = ("z", "yl", "c")
TENSOR = ("yh", "x")


def softmax_rows(scores):
    row_top = jnp.max(scores, axis=-1, keepdims=True)
    expo = jnp.exp(scores - row_top)
    return (expo / jnp.sum(expo, axis=-1, keepdims=True)).astype(jnp.bfloat16)


def rows_times_rows(left, right):
    return lax.dot_general(
        left, right, (((1,), (1,)), ((), ())), preferred_element_type=jnp.float32
    )


def attention_kernel(table_ref, query_ref, memory_ref, nbr_ref, after_ref, out_ref):
    del after_ref
    stretches, per_stretch = table_ref.shape
    pieces = nbr_ref.shape[0] // (stretches * per_stretch)
    heads = query_ref.shape[1] // HD
    for u in range(stretches):
        rows = slice(u * STRETCH, (u + 1) * STRETCH)
        places = [pl.ds(table_ref[u, j] * pieces, pieces) for j in range(per_stretch)]
        for h in range(heads):
            cols = slice(h * HD, (h + 1) * HD)
            nbr_query, nbr_key, nbr_value = (
                jnp.concatenate(
                    [nbr_ref[place, kind, :, cols].reshape(NBLEN, HD) for place in places],
                    axis=0,
                )
                for kind in range(3)
            )
            enc_probs = softmax_rows(
                rows_times_rows(nbr_query, memory_ref[0, rows, cols]) * SCALE
            )
            encoded = nbr_value.astype(jnp.float32) + jnp.dot(
                enc_probs, memory_ref[1, rows, cols], preferred_element_type=jnp.float32
            )
            encoded = encoded.astype(jnp.bfloat16)
            dec_probs = softmax_rows(
                rows_times_rows(query_ref[rows, cols], nbr_key) * SCALE
            )
            context = jnp.dot(dec_probs, encoded, preferred_element_type=jnp.float32)
            context = context.astype(jnp.bfloat16)
            for copy in range(out_ref.shape[0]):
                out_ref[copy, rows, cols] = context


VMEM = pl.BlockSpec(memory_space=pltpu.VMEM)
ANY = pl.BlockSpec(memory_space=pl.ANY)
PARAMS = pltpu.CompilerParams(vmem_limit_bytes=32 * 2**20)


def attention(table, query, memory, neighbours, copies, after):
    return pl.pallas_call(
        attention_kernel,
        out_shape=jax.ShapeDtypeStruct((copies, *query.shape), jnp.bfloat16),
        in_specs=[pl.BlockSpec(memory_space=pltpu.SMEM)] + [VMEM] * 3 + [ANY],
        out_specs=VMEM,
        compiler_params=PARAMS,
    )(table, query, memory, neighbours, after)


def pack_kernel(query_ref, key_ref, value_ref, out_ref):
    groups, _, _, span = out_ref.shape
    for kind, ref in enumerate((query_ref, key_ref, value_ref)):
        for g in range(groups):
            out_ref[g, kind] = ref[:, g * span : (g + 1) * span]


def pack(query, key, value, groups):
    rows, cols = query.shape
    return pl.pallas_call(
        pack_kernel,
        out_shape=jax.ShapeDtypeStruct((groups, 3, rows, cols // groups), query.dtype),
        in_specs=[VMEM] * 3,
        out_specs=VMEM,
        compiler_params=PARAMS,
    )(query, key, value)


def fold_kernel(weight_ref, out_ref):
    eighths, quarter, width = out_ref.shape
    part = weight_ref.shape[1] // eighths
    for e in range(eighths):
        cols = slice(e * part, (e + 1) * part)
        out_ref[e] = jnp.concatenate(
            [weight_ref[k * quarter : (k + 1) * quarter, cols] for k in range(width // part)],
            axis=1,
        )


def fold(weight, eighths):
    rows, cols = weight.shape
    part = cols // eighths
    return pl.pallas_call(
        fold_kernel,
        out_shape=jax.ShapeDtypeStruct((eighths, rows * part // HD, HD), weight.dtype),
        in_specs=[VMEM],
        out_specs=VMEM,
        compiler_params=PARAMS,
    )(weight)


def regroup_kernel(folded_ref, out_ref):
    senders, quarters, quarter, width = folded_ref.shape
    part = width // 4
    for x in range(quarters):
        for k in range(2):
            out_ref[x, k * quarter : (k + 1) * quarter] = jnp.concatenate(
                [
                    folded_ref[s, x, :, at * part : (at + 1) * part]
                    for at in (k, 2 + k)
                    for s in range(senders)
                ],
                axis=1,
            )


def regroup(folded):
    _, quarters, quarter, width = folded.shape
    return pl.pallas_call(
        regroup_kernel,
        out_shape=jax.ShapeDtypeStruct((quarters, 2 * quarter, width), folded.dtype),
        in_specs=[VMEM],
        out_specs=VMEM,
        compiler_params=PARAMS,
    )(folded)


def stack_kernel(*refs):
    out_ref = refs[-1]
    place = 0
    quarters = out_ref.shape[1]
    for ref in refs[:-1]:
        count = ref.shape[0]
        out_ref[place // quarters, pl.ds(place % quarters, count)] = ref[...]
        place += count


def stack(quarters, *values):
    count = sum(value.shape[0] for value in values) // quarters
    return pl.pallas_call(
        stack_kernel,
        out_shape=jax.ShapeDtypeStruct(
            (count, quarters, *values[0].shape[1:]), values[0].dtype
        ),
        in_specs=[VMEM] * len(values),
        out_specs=VMEM,
        compiler_params=PARAMS,
    )(*values)


def project_kernel(plane_ref, context_ref, near_ref, far_ref, near_sib_ref, far_sib_ref, out_ref):
    plane = plane_ref[0]
    sides, quarters, tokens, span = context_ref.shape
    width = near_ref.shape[-1]
    middle, half, part = width // 2, tokens // 2, width // 4
    blocks = [(near_ref, near_sib_ref, i) for i in range(near_ref.shape[0])]
    blocks += [(far_ref, far_sib_ref, i) for i in range(far_ref.shape[0])]
    planes = len(blocks)
    left = [
        jnp.concatenate([context_ref[s, x] for s in range(sides)], axis=0)
        for x in range(quarters)
    ]

    def rows_of(index, x):
        own_ref, sib_ref, i = blocks[index]
        own, sib = own_ref[i, x], sib_ref[i, x]
        upper = jnp.concatenate([own[:, :middle], sib[:, :middle]], axis=1)
        lower = jnp.concatenate([own[:, middle:], sib[:, middle:]], axis=1)
        return jnp.concatenate([upper, lower], axis=0)

    for pair in range(planes // 2):
        total = None
        for x in range(quarters):
            right = jnp.concatenate([rows_of(2 * pair, x), rows_of(2 * pair + 1, x)], axis=1)
            term = jnp.dot(left[x], right, preferred_element_type=jnp.float32)
            total = term if total is None else total + term
        total = total.astype(jnp.bfloat16)
        for s in range(sides):
            upper = total[s * tokens : s * tokens + half]
            lower = total[s * tokens + half : (s + 1) * tokens]
            for i in range(2):
                target = lax.rem(plane + OFFSETS[2 * pair + i] + planes, planes)
                for piece in range(2):
                    own = slice(i * width + piece * part, i * width + (piece + 1) * part)
                    sib = slice(own.start + middle, own.stop + middle)
                    out_ref[s, 2 * target + piece] = jnp.concatenate(
                        [upper[:, own], upper[:, sib], lower[:, own], lower[:, sib]], axis=1
                    )


def project(plane, context, near, far, near_sib, far_sib):
    sides, _, tokens, _ = context.shape
    planes = near.shape[0] + far.shape[0]
    return pl.pallas_call(
        project_kernel,
        out_shape=jax.ShapeDtypeStruct(
            (sides, 2 * planes, tokens // 2, near.shape[-1]), jnp.bfloat16
        ),
        in_specs=[pl.BlockSpec(memory_space=pltpu.SMEM)] + [VMEM] * 5,
        out_specs=VMEM,
        compiler_params=PARAMS,
    )(plane, context, near, far, near_sib, far_sib)


def add_kernel(core_ref, partial_ref, out_ref):
    sides, senders, quarters, half, width = partial_ref.shape
    middle, part = width // 2, width // 4
    for s in range(sides):
        sums = []
        for x in range(quarters):
            total = partial_ref[s, 0, x].astype(jnp.float32)
            for sender in range(1, senders):
                total += partial_ref[s, sender, x].astype(jnp.float32)
            sums.append(total.astype(jnp.bfloat16))
        for side in range(2):
            core = core_ref[0] if side == 0 else 1 - core_ref[0]
            cols = pl.ds(pl.multiple_of((core * sides + s) * width, width), width)
            for low in range(2):
                at = low * middle + side * part
                out_ref[low * half : (low + 1) * half, cols] = jnp.concatenate(
                    [one[:, at : at + part] for one in sums], axis=1
                )


def add(core, partial):
    sides, _, quarters, half, width = partial.shape
    return pl.pallas_call(
        add_kernel,
        out_shape=jax.ShapeDtypeStruct((2 * half, sides * quarters * width // 2), jnp.bfloat16),
        in_specs=[pl.BlockSpec(memory_space=pltpu.SMEM), VMEM],
        out_specs=VMEM,
        compiler_params=PARAMS,
    )(core, partial)


def exchange(value, axes):
    return lax.all_to_all(value, axes, split_axis=0, concat_axis=0, tiled=True)


OFFSETS = (0, -1, 1, -2, 2, -3, 3, 4)


def ring(value, axis, size):
    up = [(i, (i + 1) % size) for i in range(size)]
    down = [(i, (i - 1) % size) for i in range(size)]
    behind, ahead = [value], [value]
    for _ in range(size // 2 - 1):
        behind.append(lax.ppermute(behind[-1], axis, up))
        ahead.append(lax.ppermute(ahead[-1], axis, down))
    half = value.shape[0] // 2
    top = lax.ppermute(behind[-1][:half], axis, up)
    low = lax.ppermute(ahead[-1][half:], axis, down)
    near = stack(len(value), value, behind[1], ahead[1], behind[2], ahead[2], behind[3], ahead[3])
    far = stack(len(value), top, low)
    return near, far


def local(
    decoder_query,
    decoder_memory,
    neighbour_query,
    neighbour_key,
    neighbour_value,
    neighbour_table,
    output_weight,
    *,
    groups,
):
    folded = exchange(fold(output_weight, 8), ("yl", "x"))
    near, far = ring(regroup(folded.reshape(2, 4, *folded.shape[1:])), "z", 8)
    swap = [(0, 1), (1, 0)]
    near_sib, far_sib = lax.ppermute(near, "c", swap), lax.ppermute(far, "c", swap)

    neighbours = pack(neighbour_query, neighbour_key, neighbour_value, groups)
    neighbours = exchange(neighbours, TENSOR)
    context = attention(neighbour_table, decoder_query, decoder_memory, neighbours, 8, near)
    context = exchange(context, ("yl", "x"))
    context = context.reshape(2, 4, *context.shape[1:])
    plane = lax.axis_index("z").astype(jnp.int32).reshape(1)
    partial = project(plane, context, near, far, near_sib, far_sib)
    shape = partial.shape
    partial = exchange(partial.reshape(2 * groups, *shape[2:]), ("yl", "yh", "x"))
    core = lax.axis_index("c").astype(jnp.int32).reshape(1)
    return add(core, partial.reshape(2, 4, 4, *shape[2:]))


def solution(mesh):
    groups = mesh.shape["tensor"]
    inner = Mesh(mesh.devices.reshape(8, 2, 2, 4, 4), AXES)
    return jax.shard_map(
        functools.partial(local, groups=groups),
        mesh=inner,
        in_specs=(
            P(DP, TENSOR),
            P(None, DP, TENSOR),
            P(AXES, None),
            P(AXES, None),
            P(AXES, None),
            P(DP, None),
            P(TENSOR, DP),
        ),
        out_specs=P(DP, TENSOR),
        check_vma=False,
    )
```

```python
import functools
import math

import jax
import jax.numpy as jnp
from jax import lax
from jax.experimental import pallas as pl
from jax.experimental.pallas import tpu as pltpu
from jax.sharding import Mesh
from jax.sharding import PartitionSpec as P

HD = 128
STRETCH = 64
NBLEN = 128
SCALE = 1.0 / math.sqrt(HD)

AXES = ("z", "yl", "c", "yh", "x")
DP = ("z", "yl", "c")
TENSOR = ("yh", "x")


def softmax_rows(scores):
    row_top = jnp.max(scores, axis=-1, keepdims=True)
    expo = jnp.exp(scores - row_top)
    return (expo / jnp.sum(expo, axis=-1, keepdims=True)).astype(jnp.bfloat16)


def rows_times_rows(left, right):
    return lax.dot_general(
        left, right, (((1,), (1,)), ((), ())), preferred_element_type=jnp.float32
    )


def attention_kernel(table_ref, query_ref, memory_ref, nbr_ref, *refs):
    out_ref = refs[-1]
    stretches, per_stretch = table_ref.shape
    pieces = nbr_ref.shape[0] // (stretches * per_stretch)
    heads = query_ref.shape[1] // HD
    for u in range(stretches):
        rows = slice(u * STRETCH, (u + 1) * STRETCH)
        places = [pl.ds(table_ref[u, j] * pieces, pieces) for j in range(per_stretch)]
        for h in range(heads):
            cols = slice(h * HD, (h + 1) * HD)
            nbr_query, nbr_key, nbr_value = (
                jnp.concatenate(
                    [nbr_ref[place, kind, :, cols].reshape(NBLEN, HD) for place in places],
                    axis=0,
                )
                for kind in range(3)
            )
            enc_probs = softmax_rows(
                rows_times_rows(nbr_query, memory_ref[0, rows, cols]) * SCALE
            )
            encoded = nbr_value.astype(jnp.float32) + jnp.dot(
                enc_probs, memory_ref[1, rows, cols], preferred_element_type=jnp.float32
            )
            encoded = encoded.astype(jnp.bfloat16)
            dec_probs = softmax_rows(
                rows_times_rows(query_ref[rows, cols], nbr_key) * SCALE
            )
            context = jnp.dot(dec_probs, encoded, preferred_element_type=jnp.float32)
            out_ref[rows, cols] = context.astype(jnp.bfloat16)


VMEM = pl.BlockSpec(memory_space=pltpu.VMEM)
ANY = pl.BlockSpec(memory_space=pl.ANY)
HBM = pl.BlockSpec(memory_space=pltpu.HBM)
PARAMS = pltpu.CompilerParams(vmem_limit_bytes=16 * 2**20)


def attention(table, query, memory, neighbours, after):
    return pl.pallas_call(
        attention_kernel,
        out_shape=jax.ShapeDtypeStruct(query.shape, jnp.bfloat16),
        in_specs=[pl.BlockSpec(memory_space=pltpu.SMEM)] + [VMEM] * 3 + [ANY] * len(after),
        out_specs=VMEM,
        compiler_params=PARAMS,
    )(table, query, memory, neighbours, *after)


def repeat_kernel(value_ref, *refs):
    out_ref, sems = refs[-2:]
    copies = [
        pltpu.make_async_copy(value_ref, out_ref.at[i], sems.at[i]) for i in range(out_ref.shape[0])
    ]
    for copy in copies:
        copy.start()
    for copy in copies:
        copy.wait()


def repeat(value, count, after):
    return pl.pallas_call(
        repeat_kernel,
        out_shape=jax.ShapeDtypeStruct((count, *value.shape), value.dtype),
        in_specs=[VMEM] + [ANY] * len(after),
        out_specs=HBM,
        scratch_shapes=[pltpu.SemaphoreType.DMA((count,))],
        compiler_params=PARAMS,
    )(value, *after)


def pack_kernel(query_ref, key_ref, value_ref, out_ref):
    groups, _, _, span = out_ref.shape
    for kind, ref in enumerate((query_ref, key_ref, value_ref)):
        for g in range(groups):
            out_ref[g, kind] = ref[:, g * span : (g + 1) * span]


def pack(query, key, value, groups):
    rows, cols = query.shape
    return pl.pallas_call(
        pack_kernel,
        out_shape=jax.ShapeDtypeStruct((groups, 3, rows, cols // groups), query.dtype),
        in_specs=[VMEM] * 3,
        out_specs=VMEM,
        compiler_params=PARAMS,
    )(query, key, value)


def fold_kernel(weight_ref, out_ref):
    eighths, quarter, width = out_ref.shape
    part = weight_ref.shape[1] // eighths
    for e in range(eighths):
        cols = slice(e * part, (e + 1) * part)
        out_ref[e] = jnp.concatenate(
            [weight_ref[k * quarter : (k + 1) * quarter, cols] for k in range(width // part)],
            axis=1,
        )


def fold(weight, eighths):
    rows, cols = weight.shape
    part = cols // eighths
    return pl.pallas_call(
        fold_kernel,
        out_shape=jax.ShapeDtypeStruct((eighths, rows * part // HD, HD), weight.dtype),
        in_specs=[VMEM],
        out_specs=VMEM,
        compiler_params=PARAMS,
    )(weight)


def regroup_kernel(folded_ref, out_ref):
    senders, quarters, quarter, width = folded_ref.shape
    part = width // 4
    for x in range(quarters):
        for k in range(2):
            out_ref[x, k * quarter : (k + 1) * quarter] = jnp.concatenate(
                [
                    folded_ref[s, x, :, at * part : (at + 1) * part]
                    for at in (k, 2 + k)
                    for s in range(senders)
                ],
                axis=1,
            )


def regroup(folded):
    _, quarters, quarter, width = folded.shape
    return pl.pallas_call(
        regroup_kernel,
        out_shape=jax.ShapeDtypeStruct((quarters, 2 * quarter, width), folded.dtype),
        in_specs=[VMEM],
        out_specs=VMEM,
        compiler_params=PARAMS,
    )(folded)


TOGETHER = 4


def stack_kernel(*refs):
    count = (len(refs) - 1) * TOGETHER // (TOGETHER + 1)
    for i in range(count):
        refs[count + 1 + i // TOGETHER][i % TOGETHER] = refs[i][...]


def stack(blocks, after):
    shape = jax.ShapeDtypeStruct((TOGETHER, *blocks[0].shape), blocks[0].dtype)
    outs = len(blocks) // TOGETHER
    return pl.pallas_call(
        stack_kernel,
        out_shape=[shape] * outs,
        in_specs=[VMEM] * len(blocks) + [ANY],
        out_specs=[VMEM] * outs,
        compiler_params=PARAMS,
    )(*blocks, after)


def project_kernel(plane_ref, context_ref, *refs):
    out_ref = refs[-1]
    stacks = len(refs) // 2
    plane = plane_ref[0]
    sides, quarters, tokens, span = context_ref.shape
    width = refs[0].shape[-1]
    middle, half, part = width // 2, tokens // 2, width // 4
    planes = TOGETHER * stacks
    left = [
        jnp.concatenate([context_ref[s, x] for s in range(sides)], axis=0)
        for x in range(quarters)
    ]

    def rows_of(index, x):
        own = refs[index // TOGETHER][index % TOGETHER, x]
        sib = refs[stacks + index // TOGETHER][index % TOGETHER, x]
        upper = jnp.concatenate([own[:, :middle], sib[:, :middle]], axis=1)
        lower = jnp.concatenate([own[:, middle:], sib[:, middle:]], axis=1)
        return jnp.concatenate([upper, lower], axis=0)

    for pair in range(planes // 2):
        total = None
        for x in range(quarters):
            right = jnp.concatenate([rows_of(2 * pair, x), rows_of(2 * pair + 1, x)], axis=1)
            term = jnp.dot(left[x], right, preferred_element_type=jnp.float32)
            total = term if total is None else total + term
        total = total.astype(jnp.bfloat16)
        for s in range(sides):
            upper = total[s * tokens : s * tokens + half]
            lower = total[s * tokens + half : (s + 1) * tokens]
            for i in range(2):
                target = lax.rem(plane + OFFSETS[2 * pair + i] + planes, planes)
                for piece in range(2):
                    own = slice(i * width + piece * part, i * width + (piece + 1) * part)
                    sib = slice(own.start + middle, own.stop + middle)
                    out_ref[s, 2 * target + piece] = jnp.concatenate(
                        [upper[:, own], upper[:, sib], lower[:, own], lower[:, sib]], axis=1
                    )


def project(plane, context, own, sib):
    sides, _, tokens, _ = context.shape
    return pl.pallas_call(
        project_kernel,
        out_shape=jax.ShapeDtypeStruct(
            (sides, 2 * TOGETHER * len(own), tokens // 2, own[0].shape[-1]), jnp.bfloat16
        ),
        in_specs=[pl.BlockSpec(memory_space=pltpu.SMEM)] + [VMEM] * (1 + len(own) + len(sib)),
        out_specs=VMEM,
        compiler_params=PARAMS,
    )(plane, context, *own, *sib)


def add_kernel(core_ref, partial_ref, out_ref):
    sides, senders, quarters, half, width = partial_ref.shape
    middle, part = width // 2, width // 4
    for s in range(sides):
        sums = []
        for x in range(quarters):
            total = partial_ref[s, 0, x].astype(jnp.float32)
            for sender in range(1, senders):
                total += partial_ref[s, sender, x].astype(jnp.float32)
            sums.append(total.astype(jnp.bfloat16))
        for side in range(2):
            core = core_ref[0] if side == 0 else 1 - core_ref[0]
            cols = pl.ds(pl.multiple_of((core * sides + s) * width, width), width)
            for low in range(2):
                at = low * middle + side * part
                out_ref[low * half : (low + 1) * half, cols] = jnp.concatenate(
                    [one[:, at : at + part] for one in sums], axis=1
                )


def add(core, partial):
    sides, _, quarters, half, width = partial.shape
    return pl.pallas_call(
        add_kernel,
        out_shape=jax.ShapeDtypeStruct((2 * half, sides * quarters * width // 2), jnp.bfloat16),
        in_specs=[pl.BlockSpec(memory_space=pltpu.SMEM), VMEM],
        out_specs=VMEM,
        compiler_params=PARAMS,
    )(core, partial)


def exchange(value, axes):
    return lax.all_to_all(value, axes, split_axis=0, concat_axis=0, tiled=True)


OFFSETS = (0, -1, 1, -2, 2, -3, 3, -4)


def ring(value, axis, size):
    up = [(i, (i + 1) % size) for i in range(size)]
    down = [(i, (i - 1) % size) for i in range(size)]
    blocks, behind, ahead = [value], value, value
    for _ in range(size // 2 - 1):
        behind = lax.ppermute(behind, axis, up)
        ahead = lax.ppermute(ahead, axis, down)
        blocks += [behind, ahead]
    return blocks + [lax.ppermute(behind, axis, up)]


def local(
    decoder_query,
    decoder_memory,
    neighbour_query,
    neighbour_key,
    neighbour_value,
    neighbour_table,
    output_weight,
    *,
    groups,
):
    folded = exchange(fold(output_weight, 8), ("yl", "x"))
    blocks = ring(regroup(folded.reshape(2, 4, *folded.shape[1:])), "z", 8)

    neighbours = pack(neighbour_query, neighbour_key, neighbour_value, groups)
    neighbours = exchange(neighbours, TENSOR)
    table = neighbour_table & 3
    context = attention(table, decoder_query, decoder_memory, neighbours, blocks[-3:-1])
    context = repeat(context, 8, blocks[-1:])
    own = stack(blocks, context)
    sib = [lax.ppermute(block, "c", [(0, 1), (1, 0)]) for block in own]
    context = exchange(context, ("yl", "x"))
    context = context.reshape(2, 4, *context.shape[1:])
    plane = lax.axis_index("z").astype(jnp.int32).reshape(1)
    partial = project(plane, context, own, sib)
    shape = partial.shape
    partial = exchange(partial.reshape(2 * groups, *shape[2:]), ("yl", "yh", "x"))
    core = lax.axis_index("c").astype(jnp.int32).reshape(1)
    return add(core, partial.reshape(2, 4, 4, *shape[2:]))


def solution(mesh):
    groups = mesh.shape["tensor"]
    inner = Mesh(mesh.devices.reshape(8, 2, 2, 4, 4), AXES)
    return jax.shard_map(
        functools.partial(local, groups=groups),
        mesh=inner,
        in_specs=(
            P(DP, TENSOR),
            P(None, DP, TENSOR),
            P(AXES, None),
            P(AXES, None),
            P(AXES, None),
            P(DP, None),
            P(TENSOR, DP),
        ),
        out_specs=P(DP, TENSOR),
        check_vma=False,
    )
```

```python
import math

import jax
import jax.numpy as jnp
from jax import lax
from jax.experimental import pallas as pl
from jax.experimental.pallas import tpu as pltpu
from jax.sharding import Mesh
from jax.sharding import PartitionSpec as P

HD = 128
STRETCH = 64
NBLEN = 128
SCALE = 1.0 / math.sqrt(HD)

AXES = ("z", "yl", "c", "yh", "x")
DP = ("z", "yl", "c")
TENSOR = ("yh", "x")


def softmax_rows(scores):
    row_top = jnp.max(scores, axis=-1, keepdims=True)
    expo = jnp.exp(scores - row_top)
    return (expo / jnp.sum(expo, axis=-1, keepdims=True)).astype(jnp.bfloat16)


def rows_times_rows(left, right):
    return lax.dot_general(
        left, right, (((1,), (1,)), ((), ())), preferred_element_type=jnp.float32
    )


def attention_kernel(table_ref, query_ref, memory_ref, nbr_ref, *refs):
    out_ref = refs[-1]
    stretches, per_stretch = table_ref.shape
    heads = query_ref.shape[1] // HD
    for u in range(stretches):
        rows = slice(u * STRETCH, (u + 1) * STRETCH)
        places = [table_ref[u, j] for j in range(per_stretch)]
        for h in range(heads):
            cols = slice(h * HD, (h + 1) * HD)
            nbr_query, nbr_key, nbr_value = (
                jnp.concatenate(
                    [
                        nbr_ref[x, place, kind, :, cols]
                        for place in places
                        for x in range(nbr_ref.shape[0])
                    ],
                    axis=0,
                )
                for kind in range(3)
            )
            enc_probs = softmax_rows(
                rows_times_rows(nbr_query, memory_ref[0, rows, cols]) * SCALE
            )
            encoded = nbr_value.astype(jnp.float32) + jnp.dot(
                enc_probs, memory_ref[1, rows, cols], preferred_element_type=jnp.float32
            )
            encoded = encoded.astype(jnp.bfloat16)
            dec_probs = softmax_rows(
                rows_times_rows(query_ref[rows, cols], nbr_key) * SCALE
            )
            context = jnp.dot(dec_probs, encoded, preferred_element_type=jnp.float32)
            out_ref[rows, cols] = context.astype(jnp.bfloat16)


VMEM = pl.BlockSpec(memory_space=pltpu.VMEM)
ANY = pl.BlockSpec(memory_space=pl.ANY)
HBM = pl.BlockSpec(memory_space=pltpu.HBM)
PARAMS = pltpu.CompilerParams(vmem_limit_bytes=16 * 2**20)


def attention(table, query, memory, neighbours, after):
    return pl.pallas_call(
        attention_kernel,
        out_shape=jax.ShapeDtypeStruct(query.shape, jnp.bfloat16),
        in_specs=[pl.BlockSpec(memory_space=pltpu.SMEM)] + [VMEM] * 3 + [ANY] * len(after),
        out_specs=VMEM,
        compiler_params=PARAMS,
    )(table, query, memory, neighbours, *after)


def repeat_kernel(value_ref, *refs):
    out_ref, sems = refs[-2:]
    copies = [
        pltpu.make_async_copy(value_ref, out_ref.at[i], sems.at[i]) for i in range(out_ref.shape[0])
    ]
    for copy in copies:
        copy.start()
    for copy in copies:
        copy.wait()


def repeat(value, count, after):
    return pl.pallas_call(
        repeat_kernel,
        out_shape=jax.ShapeDtypeStruct((count, *value.shape), value.dtype),
        in_specs=[VMEM] + [ANY] * len(after),
        out_specs=HBM,
        scratch_shapes=[pltpu.SemaphoreType.DMA((count,))],
        compiler_params=PARAMS,
    )(value, *after)


def pack_kernel(query_ref, key_ref, value_ref, out_ref):
    quarters, highs, _, _, span = out_ref.shape
    for kind, ref in enumerate((query_ref, key_ref, value_ref)):
        for x in range(quarters):
            for y in range(highs):
                at = (y * quarters + x) * span
                out_ref[x, y, kind] = ref[:, at : at + span]


def pack(query, key, value, quarters, highs):
    rows, cols = query.shape
    span = cols // (quarters * highs)
    return pl.pallas_call(
        pack_kernel,
        out_shape=jax.ShapeDtypeStruct((quarters, highs, 3, rows, span), query.dtype),
        in_specs=[VMEM] * 3,
        out_specs=VMEM,
        compiler_params=PARAMS,
    )(query, key, value)


def fold_kernel(weight_ref, out_ref):
    eighths, quarter, width = out_ref.shape
    part = weight_ref.shape[1] // eighths
    for e in range(eighths):
        cols = slice(e * part, (e + 1) * part)
        out_ref[e] = jnp.concatenate(
            [weight_ref[k * quarter : (k + 1) * quarter, cols] for k in range(width // part)],
            axis=1,
        )


def fold(weight, eighths):
    rows, cols = weight.shape
    part = cols // eighths
    return pl.pallas_call(
        fold_kernel,
        out_shape=jax.ShapeDtypeStruct((eighths, rows * part // HD, HD), weight.dtype),
        in_specs=[VMEM],
        out_specs=VMEM,
        compiler_params=PARAMS,
    )(weight)


def regroup_kernel(folded_ref, out_ref):
    quarters, senders, quarter, width = folded_ref.shape
    part = width // 4
    for x in range(quarters):
        for k in range(2):
            out_ref[x, k * quarter : (k + 1) * quarter] = jnp.concatenate(
                [
                    folded_ref[x, s, :, at * part : (at + 1) * part]
                    for at in (k, 2 + k)
                    for s in range(senders)
                ],
                axis=1,
            )


def regroup(folded):
    quarters, _, quarter, width = folded.shape
    return pl.pallas_call(
        regroup_kernel,
        out_shape=jax.ShapeDtypeStruct((quarters, 2 * quarter, width), folded.dtype),
        in_specs=[VMEM],
        out_specs=VMEM,
        compiler_params=PARAMS,
    )(folded)


TOGETHER = 4


def stack_kernel(*refs):
    count = (len(refs) - 1) * TOGETHER // (TOGETHER + 1)
    for i in range(count):
        refs[count + 1 + i // TOGETHER][i % TOGETHER] = refs[i][...]


def stack(blocks, after):
    shape = jax.ShapeDtypeStruct((TOGETHER, *blocks[0].shape), blocks[0].dtype)
    outs = len(blocks) // TOGETHER
    return pl.pallas_call(
        stack_kernel,
        out_shape=[shape] * outs,
        in_specs=[VMEM] * len(blocks) + [ANY],
        out_specs=[VMEM] * outs,
        compiler_params=PARAMS,
    )(*blocks, after)


def project_kernel(plane_ref, context_ref, *refs):
    out_ref = refs[-1]
    stacks = len(refs) // 2
    plane = plane_ref[0]
    quarters, sides, tokens, span = context_ref.shape
    width = refs[0].shape[-1]
    middle, half, part = width // 2, tokens // 2, width // 4
    planes = TOGETHER * stacks
    left = [
        jnp.concatenate([context_ref[x, s] for s in range(sides)], axis=0)
        for x in range(quarters)
    ]

    def rows_of(index, x):
        own = refs[index // TOGETHER][index % TOGETHER, x]
        sib = refs[stacks + index // TOGETHER][index % TOGETHER, x]
        upper = jnp.concatenate([own[:, :middle], sib[:, :middle]], axis=1)
        lower = jnp.concatenate([own[:, middle:], sib[:, middle:]], axis=1)
        return jnp.concatenate([upper, lower], axis=0)

    for pair in range(planes // 2):
        total = None
        for x in range(quarters):
            right = jnp.concatenate([rows_of(2 * pair, x), rows_of(2 * pair + 1, x)], axis=1)
            term = jnp.dot(left[x], right, preferred_element_type=jnp.float32)
            total = term if total is None else total + term
        total = total.astype(jnp.bfloat16)
        for s in range(sides):
            upper = total[s * tokens : s * tokens + half]
            lower = total[s * tokens + half : (s + 1) * tokens]
            for i in range(2):
                target = lax.rem(plane + OFFSETS[2 * pair + i] + planes, planes)
                for piece in range(2):
                    own = slice(i * width + piece * part, i * width + (piece + 1) * part)
                    sib = slice(own.start + middle, own.stop + middle)
                    x = 2 * lax.rem(target, 2) + piece
                    out_ref[x, s, lax.div(target, 2)] = jnp.concatenate(
                        [upper[:, own], upper[:, sib], lower[:, own], lower[:, sib]], axis=1
                    )


def project(plane, context, own, sib):
    quarters, sides, tokens, _ = context.shape
    highs = 2 * TOGETHER * len(own) // quarters
    return pl.pallas_call(
        project_kernel,
        out_shape=jax.ShapeDtypeStruct(
            (quarters, sides, highs, tokens // 2, own[0].shape[-1]), jnp.bfloat16
        ),
        in_specs=[pl.BlockSpec(memory_space=pltpu.SMEM)] + [VMEM] * (1 + len(own) + len(sib)),
        out_specs=VMEM,
        compiler_params=PARAMS,
    )(plane, context, *own, *sib)


def add_kernel(core_ref, partial_ref, out_ref):
    quarters, sides, senders, half, width = partial_ref.shape
    middle, part = width // 2, width // 4
    together = width // (part * sides)
    for first in range(0, quarters, together):
        sums = []
        for x in range(first, first + together):
            for s in range(sides):
                total = partial_ref[x, s, 0].astype(jnp.float32)
                for sender in range(1, senders):
                    total += partial_ref[x, s, sender].astype(jnp.float32)
                sums.append(total.astype(jnp.bfloat16))
        for side in range(2):
            core = core_ref[0] if side == 0 else 1 - core_ref[0]
            at = (core * (quarters // together) + first // together) * width
            cols = pl.ds(pl.multiple_of(at, width), width)
            for low in range(2):
                at = low * middle + side * part
                out_ref[low * half : (low + 1) * half, cols] = jnp.concatenate(
                    [one[:, at : at + part] for one in sums], axis=1
                )


def add(core, partial):
    quarters, sides, _, half, width = partial.shape
    return pl.pallas_call(
        add_kernel,
        out_shape=jax.ShapeDtypeStruct((2 * half, sides * quarters * width // 2), jnp.bfloat16),
        in_specs=[pl.BlockSpec(memory_space=pltpu.SMEM), VMEM],
        out_specs=VMEM,
        compiler_params=PARAMS,
    )(core, partial)


def exchange(value, axes):
    shape = value.shape
    value = value.reshape(-1, *shape[len(axes) :])
    value = lax.all_to_all(value, axes, split_axis=0, concat_axis=0, tiled=True)
    return value.reshape(shape)


OFFSETS = (0, -1, 1, -2, 2, -3, 3, -4)


def ring(value, axis, size):
    up = [(i, (i + 1) % size) for i in range(size)]
    down = [(i, (i - 1) % size) for i in range(size)]
    blocks, behind, ahead = [value], value, value
    for _ in range(size // 2 - 1):
        behind = lax.ppermute(behind, axis, up)
        ahead = lax.ppermute(ahead, axis, down)
        blocks += [behind, ahead]
    return blocks + [lax.ppermute(behind, axis, up)]


def local(
    decoder_query,
    decoder_memory,
    neighbour_query,
    neighbour_key,
    neighbour_value,
    neighbour_table,
    output_weight,
):
    folded = fold(output_weight, 8)
    folded = exchange(folded.reshape(4, 2, *folded.shape[1:]), ("x", "yl"))
    blocks = ring(regroup(folded), "z", 8)

    neighbours = pack(neighbour_query, neighbour_key, neighbour_value, 4, 4)
    neighbours = exchange(neighbours, ("x", "yh"))
    table = neighbour_table & 3
    context = attention(table, decoder_query, decoder_memory, neighbours, blocks[-3:-1])
    context = repeat(context, 8, blocks[-1:])
    own = stack(blocks, context)
    sib = [lax.ppermute(block, "c", [(0, 1), (1, 0)]) for block in own]
    context = exchange(context.reshape(4, 2, *context.shape[1:]), ("x", "yl"))
    plane = lax.axis_index("z").astype(jnp.int32).reshape(1)
    partial = exchange(project(plane, context, own, sib), ("x", "yl", "yh"))
    core = lax.axis_index("c").astype(jnp.int32).reshape(1)
    return add(core, partial)


def solution(mesh):
    inner = Mesh(mesh.devices.reshape(8, 2, 2, 4, 4), AXES)
    return jax.shard_map(
        local,
        mesh=inner,
        in_specs=(
            P(DP, TENSOR),
            P(None, DP, TENSOR),
            P(AXES, None),
            P(AXES, None),
            P(AXES, None),
            P(DP, None),
            P(TENSOR, DP),
        ),
        out_specs=P(DP, TENSOR),
        check_vma=False,
    )
```

```python
import math

import jax
import jax.numpy as jnp
from jax import lax
from jax.experimental import pallas as pl
from jax.experimental.pallas import tpu as pltpu
from jax.sharding import Mesh
from jax.sharding import PartitionSpec as P

HD = 128
STRETCH = 64
NBLEN = 128
SCALE = 1.0 / math.sqrt(HD)

AXES = ("z", "yl", "c", "yh", "x")
DP = ("z", "yl", "c")
TENSOR = ("yh", "x")


def softmax_rows(scores):
    row_top = jnp.max(scores, axis=-1, keepdims=True)
    expo = jnp.exp(scores - row_top)
    return (expo / jnp.sum(expo, axis=-1, keepdims=True)).astype(jnp.bfloat16)


def rows_times_rows(left, right):
    return lax.dot_general(
        left, right, (((1,), (1,)), ((), ())), preferred_element_type=jnp.float32
    )


def attention_kernel(table_ref, query_ref, memory_ref, nbr_ref, *refs):
    out_ref = refs[-1]
    stretches, per_stretch = table_ref.shape
    heads = query_ref.shape[1] // HD
    for u in range(stretches):
        rows = slice(u * STRETCH, (u + 1) * STRETCH)
        places = [table_ref[u, j] for j in range(per_stretch)]
        for h in range(heads):
            cols = slice(h * HD, (h + 1) * HD)
            nbr_query, nbr_key, nbr_value = (
                jnp.concatenate(
                    [
                        nbr_ref[x, place, kind, :, cols]
                        for place in places
                        for x in range(nbr_ref.shape[0])
                    ],
                    axis=0,
                )
                for kind in range(3)
            )
            enc_probs = softmax_rows(
                rows_times_rows(nbr_query, memory_ref[0, rows, cols]) * SCALE
            )
            encoded = nbr_value.astype(jnp.float32) + jnp.dot(
                enc_probs, memory_ref[1, rows, cols], preferred_element_type=jnp.float32
            )
            encoded = encoded.astype(jnp.bfloat16)
            dec_probs = softmax_rows(
                rows_times_rows(query_ref[rows, cols], nbr_key) * SCALE
            )
            context = jnp.dot(dec_probs, encoded, preferred_element_type=jnp.float32)
            out_ref[rows, cols] = context.astype(jnp.bfloat16)


VMEM = pl.BlockSpec(memory_space=pltpu.VMEM)
ANY = pl.BlockSpec(memory_space=pl.ANY)
HBM = pl.BlockSpec(memory_space=pltpu.HBM)
PARAMS = pltpu.CompilerParams(vmem_limit_bytes=16 * 2**20)
WIDE = pltpu.CompilerParams(vmem_limit_bytes=60 * 2**20)


def attention(table, query, memory, neighbours, after):
    return pl.pallas_call(
        attention_kernel,
        out_shape=jax.ShapeDtypeStruct(query.shape, jnp.bfloat16),
        in_specs=[pl.BlockSpec(memory_space=pltpu.SMEM)] + [VMEM] * 3 + [ANY] * len(after),
        out_specs=VMEM,
        compiler_params=PARAMS,
    )(table, query, memory, neighbours, *after)


def repeat_kernel(value_ref, *refs):
    out_ref, sems = refs[-2:]
    copies = [
        pltpu.make_async_copy(value_ref, out_ref.at[i], sems.at[i]) for i in range(out_ref.shape[0])
    ]
    for copy in copies:
        copy.start()
    for copy in copies:
        copy.wait()


def repeat(value, count, after):
    return pl.pallas_call(
        repeat_kernel,
        out_shape=jax.ShapeDtypeStruct((count, *value.shape), value.dtype),
        in_specs=[VMEM] + [ANY] * len(after),
        out_specs=HBM,
        scratch_shapes=[pltpu.SemaphoreType.DMA((count,))],
        compiler_params=PARAMS,
    )(value, *after)


def pack_kernel(query_ref, key_ref, value_ref, out_ref, held, packed, in_sems, out_sems):
    quarters, highs, _, _, span = out_ref.shape
    loads = [
        pltpu.make_async_copy(ref, held.at[kind], in_sems.at[kind])
        for kind, ref in enumerate((query_ref, key_ref, value_ref))
    ]
    stores = [
        pltpu.make_async_copy(
            packed.at[x, :, kind], out_ref.at[x, :, kind], out_sems.at[x, kind]
        )
        for kind in range(len(loads))
        for x in range(quarters)
    ]
    for load in loads:
        load.start()
    for kind, load in enumerate(loads):
        load.wait()
        for x in range(quarters):
            for y in range(highs):
                at = (y * quarters + x) * span
                packed[x, y, kind] = held[kind, :, at : at + span]
            stores[kind * quarters + x].start()
    for store in stores:
        store.wait()


def pack(query, key, value, quarters, highs):
    rows, cols = query.shape
    span = cols // (quarters * highs)
    shape = (quarters, highs, 3, rows, span)
    return pl.pallas_call(
        pack_kernel,
        out_shape=jax.ShapeDtypeStruct(shape, query.dtype),
        in_specs=[HBM] * 3,
        out_specs=HBM,
        scratch_shapes=[
            pltpu.VMEM((3, rows, cols), query.dtype),
            pltpu.VMEM(shape, query.dtype),
            pltpu.SemaphoreType.DMA((3,)),
            pltpu.SemaphoreType.DMA((quarters, 3)),
        ],
        compiler_params=WIDE,
    )(query, key, value)


def fold_kernel(weight_ref, out_ref):
    eighths, quarter, width = out_ref.shape
    part = weight_ref.shape[1] // eighths
    for e in range(eighths):
        cols = slice(e * part, (e + 1) * part)
        out_ref[e] = jnp.concatenate(
            [weight_ref[k * quarter : (k + 1) * quarter, cols] for k in range(width // part)],
            axis=1,
        )


def fold(weight, eighths):
    rows, cols = weight.shape
    part = cols // eighths
    return pl.pallas_call(
        fold_kernel,
        out_shape=jax.ShapeDtypeStruct((eighths, rows * part // HD, HD), weight.dtype),
        in_specs=[VMEM],
        out_specs=VMEM,
        compiler_params=PARAMS,
    )(weight)


def regroup_kernel(folded_ref, out_ref):
    quarters, senders, quarter, width = folded_ref.shape
    part = width // 4
    for x in range(quarters):
        for k in range(2):
            out_ref[x, k * quarter : (k + 1) * quarter] = jnp.concatenate(
                [
                    folded_ref[x, s, :, at * part : (at + 1) * part]
                    for at in (k, 2 + k)
                    for s in range(senders)
                ],
                axis=1,
            )


def regroup(folded):
    quarters, _, quarter, width = folded.shape
    return pl.pallas_call(
        regroup_kernel,
        out_shape=jax.ShapeDtypeStruct((quarters, 2 * quarter, width), folded.dtype),
        in_specs=[VMEM],
        out_specs=VMEM,
        compiler_params=PARAMS,
    )(folded)


TOGETHER = 4


def stack_kernel(*refs):
    count = (len(refs) - 1) * TOGETHER // (TOGETHER + 1)
    for i in range(count):
        refs[count + 1 + i // TOGETHER][i % TOGETHER] = refs[i][...]


def stack(blocks, after):
    shape = jax.ShapeDtypeStruct((TOGETHER, *blocks[0].shape), blocks[0].dtype)
    outs = len(blocks) // TOGETHER
    return pl.pallas_call(
        stack_kernel,
        out_shape=[shape] * outs,
        in_specs=[VMEM] * len(blocks) + [ANY],
        out_specs=[VMEM] * outs,
        compiler_params=PARAMS,
    )(*blocks, after)


def project_kernel(plane_ref, context_ref, *refs):
    out_ref = refs[-1]
    stacks = len(refs) // 2
    plane = plane_ref[0]
    quarters, sides, tokens, span = context_ref.shape
    width = refs[0].shape[-1]
    middle, half, part = width // 2, tokens // 2, width // 4
    planes = TOGETHER * stacks
    left = [
        jnp.concatenate([context_ref[x, s] for s in range(sides)], axis=0)
        for x in range(quarters)
    ]

    def rows_of(index, x):
        own = refs[index // TOGETHER][index % TOGETHER, x]
        sib = refs[stacks + index // TOGETHER][index % TOGETHER, x]
        upper = jnp.concatenate([own[:, :middle], sib[:, :middle]], axis=1)
        lower = jnp.concatenate([own[:, middle:], sib[:, middle:]], axis=1)
        return jnp.concatenate([upper, lower], axis=0)

    for pair in range(planes // 2):
        total = None
        for x in range(quarters):
            right = jnp.concatenate([rows_of(2 * pair, x), rows_of(2 * pair + 1, x)], axis=1)
            term = jnp.dot(left[x], right, preferred_element_type=jnp.float32)
            total = term if total is None else total + term
        total = total.astype(jnp.bfloat16)
        for s in range(sides):
            upper = total[s * tokens : s * tokens + half]
            lower = total[s * tokens + half : (s + 1) * tokens]
            for i in range(2):
                target = lax.rem(plane + OFFSETS[2 * pair + i] + planes, planes)
                for piece in range(2):
                    own = slice(i * width + piece * part, i * width + (piece + 1) * part)
                    sib = slice(own.start + middle, own.stop + middle)
                    x = 2 * lax.rem(target, 2) + piece
                    out_ref[x, s, lax.div(target, 2)] = jnp.concatenate(
                        [upper[:, own], upper[:, sib], lower[:, own], lower[:, sib]], axis=1
                    )


def project(plane, context, own, sib):
    quarters, sides, tokens, _ = context.shape
    highs = 2 * TOGETHER * len(own) // quarters
    return pl.pallas_call(
        project_kernel,
        out_shape=jax.ShapeDtypeStruct(
            (quarters, sides, highs, tokens // 2, own[0].shape[-1]), jnp.bfloat16
        ),
        in_specs=[pl.BlockSpec(memory_space=pltpu.SMEM)] + [VMEM] * (1 + len(own) + len(sib)),
        out_specs=VMEM,
        compiler_params=PARAMS,
    )(plane, context, *own, *sib)


def add_kernel(core_ref, partial_ref, out_ref):
    quarters, sides, senders, half, width = partial_ref.shape
    middle, part = width // 2, width // 4
    together = width // (part * sides)
    for first in range(0, quarters, together):
        sums = []
        for x in range(first, first + together):
            for s in range(sides):
                total = partial_ref[x, s, 0].astype(jnp.float32)
                for sender in range(1, senders):
                    total += partial_ref[x, s, sender].astype(jnp.float32)
                sums.append(total.astype(jnp.bfloat16))
        for side in range(2):
            core = core_ref[0] if side == 0 else 1 - core_ref[0]
            at = (core * (quarters // together) + first // together) * width
            cols = pl.ds(pl.multiple_of(at, width), width)
            for low in range(2):
                at = low * middle + side * part
                out_ref[low * half : (low + 1) * half, cols] = jnp.concatenate(
                    [one[:, at : at + part] for one in sums], axis=1
                )


def add(core, partial):
    quarters, sides, _, half, width = partial.shape
    return pl.pallas_call(
        add_kernel,
        out_shape=jax.ShapeDtypeStruct((2 * half, sides * quarters * width // 2), jnp.bfloat16),
        in_specs=[pl.BlockSpec(memory_space=pltpu.SMEM), VMEM],
        out_specs=VMEM,
        compiler_params=PARAMS,
    )(core, partial)


def exchange(value, axes):
    shape = value.shape
    value = value.reshape(-1, *shape[len(axes) :])
    value = lax.all_to_all(value, axes, split_axis=0, concat_axis=0, tiled=True)
    return value.reshape(shape)


OFFSETS = (0, -1, 1, -2, 2, -3, 3, 4)


def ring(value, axis, size):
    up = [(i, (i + 1) % size) for i in range(size)]
    down = [(i, (i - 1) % size) for i in range(size)]
    blocks, behind, ahead = [value], value, value
    for _ in range(size // 2 - 1):
        behind = lax.ppermute(behind, axis, up)
        ahead = lax.ppermute(ahead, axis, down)
        blocks += [behind, ahead]
    return blocks + [lax.ppermute(ahead, axis, down)]


def local(
    decoder_query,
    decoder_memory,
    neighbour_query,
    neighbour_key,
    neighbour_value,
    neighbour_table,
    output_weight,
):
    folded = fold(output_weight, 8)
    folded = exchange(folded.reshape(4, 2, *folded.shape[1:]), ("x", "yl"))
    blocks = ring(regroup(folded), "z", 8)

    neighbours = pack(neighbour_query, neighbour_key, neighbour_value, 4, 4)
    neighbours = exchange(neighbours, ("x", "yh"))
    table = neighbour_table & 3
    context = attention(table, decoder_query, decoder_memory, neighbours, blocks[-3:-1])
    context = repeat(context, 8, blocks[-1:])
    own = stack(blocks, context)
    sib = [lax.ppermute(block, "c", [(0, 1), (1, 0)]) for block in own]
    context = exchange(context.reshape(4, 2, *context.shape[1:]), ("x", "yl"))
    plane = lax.axis_index("z").astype(jnp.int32).reshape(1)
    partial = exchange(project(plane, context, own, sib), ("x", "yl", "yh"))
    core = lax.axis_index("c").astype(jnp.int32).reshape(1)
    return add(core, partial)


def solution(mesh):
    inner = Mesh(mesh.devices.reshape(8, 2, 2, 4, 4), AXES)
    return jax.shard_map(
        local,
        mesh=inner,
        in_specs=(
            P(DP, TENSOR),
            P(None, DP, TENSOR),
            P(AXES, None),
            P(AXES, None),
            P(AXES, None),
            P(DP, None),
            P(TENSOR, DP),
        ),
        out_specs=P(DP, TENSOR),
        check_vma=False,
    )
```

```python
import math

import jax
import jax.numpy as jnp
from jax import lax
from jax.experimental import pallas as pl
from jax.experimental.pallas import tpu as pltpu
from jax.sharding import Mesh
from jax.sharding import PartitionSpec as P

HD = 128
STRETCH = 64
NBLEN = 128
SCALE = 1.0 / math.sqrt(HD)

AXES = ("z", "yl", "c", "yh", "x")
DP = ("z", "yl", "c")
TENSOR = ("yh", "x")


def softmax_rows(scores):
    row_top = jnp.max(scores, axis=-1, keepdims=True)
    expo = jnp.exp(scores - row_top)
    return (expo * (1.0 / jnp.sum(expo, axis=-1, keepdims=True))).astype(jnp.bfloat16)


def rows_times_rows(left, right):
    return lax.dot_general(
        left, right, (((1,), (1,)), ((), ())), preferred_element_type=jnp.float32
    )


def attention_kernel(table_ref, query_ref, memory_ref, nbr_ref, *refs):
    out_ref = refs[-1]
    stretches, per_stretch = table_ref.shape
    heads = query_ref.shape[1] // HD
    parts = [
        (u, slice(u * STRETCH, (u + 1) * STRETCH), slice(h * HD, (h + 1) * HD))
        for u in range(stretches)
        for h in range(heads)
    ]
    places = [[table_ref[u, j] for j in range(per_stretch)] for u in range(stretches)]

    def gathered(kind, u, cols):
        return jnp.concatenate(
            [
                nbr_ref[x, place, kind, :, cols]
                for place in places[u]
                for x in range(nbr_ref.shape[0])
            ],
            axis=0,
        )

    enc_scores = [
        rows_times_rows(gathered(0, u, cols), memory_ref[0, rows, cols]) * SCALE
        for u, rows, cols in parts
    ]
    dec_scores = [
        rows_times_rows(query_ref[rows, cols], gathered(1, u, cols)) * SCALE
        for u, rows, cols in parts
    ]
    enc_probs = [softmax_rows(scores) for scores in enc_scores]
    dec_probs = [softmax_rows(scores) for scores in dec_scores]
    encoded = [
        (
            gathered(2, u, cols).astype(jnp.float32)
            + jnp.dot(probs, memory_ref[1, rows, cols], preferred_element_type=jnp.float32)
        ).astype(jnp.bfloat16)
        for probs, (u, rows, cols) in zip(enc_probs, parts)
    ]
    for probs, values, (_, rows, cols) in zip(dec_probs, encoded, parts):
        context = jnp.dot(probs, values, preferred_element_type=jnp.float32)
        out_ref[rows, cols] = context.astype(jnp.bfloat16)


VMEM = pl.BlockSpec(memory_space=pltpu.VMEM)
ANY = pl.BlockSpec(memory_space=pl.ANY)
HBM = pl.BlockSpec(memory_space=pltpu.HBM)
PARAMS = pltpu.CompilerParams(vmem_limit_bytes=16 * 2**20)
WIDE = pltpu.CompilerParams(vmem_limit_bytes=60 * 2**20)


def attention(table, query, memory, neighbours, after):
    return pl.pallas_call(
        attention_kernel,
        out_shape=jax.ShapeDtypeStruct(query.shape, jnp.bfloat16),
        in_specs=[pl.BlockSpec(memory_space=pltpu.SMEM)] + [VMEM] * 3 + [ANY] * len(after),
        out_specs=VMEM,
        compiler_params=PARAMS,
    )(table, query, memory, neighbours, *after)


def repeat_kernel(value_ref, *refs):
    out_ref, sems = refs[-2:]
    copies = [
        pltpu.make_async_copy(value_ref, out_ref.at[i], sems.at[i]) for i in range(out_ref.shape[0])
    ]
    for copy in copies:
        copy.start()
    for copy in copies:
        copy.wait()


def repeat(value, count, after):
    return pl.pallas_call(
        repeat_kernel,
        out_shape=jax.ShapeDtypeStruct((count, *value.shape), value.dtype),
        in_specs=[VMEM] + [ANY] * len(after),
        out_specs=HBM,
        scratch_shapes=[pltpu.SemaphoreType.DMA((count,))],
        compiler_params=PARAMS,
    )(value, *after)


def pack_kernel(query_ref, key_ref, value_ref, out_ref, held, packed, in_sems, out_sems):
    quarters, highs, _, _, span = out_ref.shape
    loads = [
        pltpu.make_async_copy(ref, held.at[kind], in_sems.at[kind])
        for kind, ref in enumerate((query_ref, key_ref, value_ref))
    ]
    stores = [
        pltpu.make_async_copy(
            packed.at[x, :, kind], out_ref.at[x, :, kind], out_sems.at[x, kind]
        )
        for kind in range(len(loads))
        for x in range(quarters)
    ]
    for load in loads:
        load.start()
    for kind, load in enumerate(loads):
        load.wait()
        for x in range(quarters):
            for y in range(highs):
                at = (y * quarters + x) * span
                packed[x, y, kind] = held[kind, :, at : at + span]
            stores[kind * quarters + x].start()
    for store in stores:
        store.wait()


def pack(query, key, value, quarters, highs):
    rows, cols = query.shape
    span = cols // (quarters * highs)
    shape = (quarters, highs, 3, rows, span)
    return pl.pallas_call(
        pack_kernel,
        out_shape=jax.ShapeDtypeStruct(shape, query.dtype),
        in_specs=[HBM] * 3,
        out_specs=HBM,
        scratch_shapes=[
            pltpu.VMEM((3, rows, cols), query.dtype),
            pltpu.VMEM(shape, query.dtype),
            pltpu.SemaphoreType.DMA((3,)),
            pltpu.SemaphoreType.DMA((quarters, 3)),
        ],
        compiler_params=WIDE,
    )(query, key, value)


def fold_kernel(weight_ref, out_ref):
    eighths, quarter, width = out_ref.shape
    part = weight_ref.shape[1] // eighths
    for e in range(eighths):
        cols = slice(e * part, (e + 1) * part)
        out_ref[e] = jnp.concatenate(
            [weight_ref[k * quarter : (k + 1) * quarter, cols] for k in range(width // part)],
            axis=1,
        )


def fold(weight, eighths):
    rows, cols = weight.shape
    part = cols // eighths
    return pl.pallas_call(
        fold_kernel,
        out_shape=jax.ShapeDtypeStruct((eighths, rows * part // HD, HD), weight.dtype),
        in_specs=[VMEM],
        out_specs=VMEM,
        compiler_params=PARAMS,
    )(weight)


def regroup_kernel(folded_ref, out_ref):
    quarters, senders, quarter, width = folded_ref.shape
    part = width // 4
    for x in range(quarters):
        for k in range(2):
            out_ref[x, k * quarter : (k + 1) * quarter] = jnp.concatenate(
                [
                    folded_ref[x, s, :, at * part : (at + 1) * part]
                    for at in (k, 2 + k)
                    for s in range(senders)
                ],
                axis=1,
            )


def regroup(folded):
    quarters, _, quarter, width = folded.shape
    return pl.pallas_call(
        regroup_kernel,
        out_shape=jax.ShapeDtypeStruct((quarters, 2 * quarter, width), folded.dtype),
        in_specs=[VMEM],
        out_specs=VMEM,
        compiler_params=PARAMS,
    )(folded)


TOGETHER = 4


def stack_kernel(*refs):
    count = (len(refs) - 1) * TOGETHER // (TOGETHER + 1)
    for i in range(count):
        refs[count + 1 + i // TOGETHER][i % TOGETHER] = refs[i][...]


def stack(blocks, after):
    shape = jax.ShapeDtypeStruct((TOGETHER, *blocks[0].shape), blocks[0].dtype)
    outs = len(blocks) // TOGETHER
    return pl.pallas_call(
        stack_kernel,
        out_shape=[shape] * outs,
        in_specs=[VMEM] * len(blocks) + [ANY],
        out_specs=[VMEM] * outs,
        compiler_params=PARAMS,
    )(*blocks, after)


def project_kernel(plane_ref, context_ref, *refs):
    out_ref = refs[-1]
    stacks = len(refs) // 2
    plane = plane_ref[0]
    quarters, sides, tokens, span = context_ref.shape
    width = refs[0].shape[-1]
    middle, half, part = width // 2, tokens // 2, width // 4
    planes = TOGETHER * stacks
    left = [
        jnp.concatenate([context_ref[x, s] for s in range(sides)], axis=0)
        for x in range(quarters)
    ]

    def rows_of(index, x):
        own = refs[index // TOGETHER][index % TOGETHER, x]
        sib = refs[stacks + index // TOGETHER][index % TOGETHER, x]
        upper = jnp.concatenate([own[:, :middle], sib[:, :middle]], axis=1)
        lower = jnp.concatenate([own[:, middle:], sib[:, middle:]], axis=1)
        return jnp.concatenate([upper, lower], axis=0)

    totals = []
    for pair in range(planes // 2):
        total = None
        for x in range(quarters):
            right = jnp.concatenate([rows_of(2 * pair, x), rows_of(2 * pair + 1, x)], axis=1)
            term = jnp.dot(left[x], right, preferred_element_type=jnp.float32)
            total = term if total is None else total + term
        totals.append(total.astype(jnp.bfloat16))
    for index in range(planes):
        total = totals[index // 2]
        first = index % 2 * width
        target = lax.rem(plane + OFFSETS[index] + planes, planes)
        for s in range(sides):
            upper = total[s * tokens : s * tokens + half]
            lower = total[s * tokens + half : (s + 1) * tokens]
            for piece in range(2):
                own = slice(first + piece * part, first + (piece + 1) * part)
                sib = slice(own.start + middle, own.stop + middle)
                x = 2 * lax.rem(target, 2) + piece
                out_ref[x, s, lax.div(target, 2)] = jnp.concatenate(
                    [upper[:, own], upper[:, sib], lower[:, own], lower[:, sib]], axis=1
                )


def project(plane, context, own, sib):
    quarters, sides, tokens, _ = context.shape
    highs = 2 * TOGETHER * len(own) // quarters
    return pl.pallas_call(
        project_kernel,
        out_shape=jax.ShapeDtypeStruct(
            (quarters, sides, highs, tokens // 2, own[0].shape[-1]), jnp.bfloat16
        ),
        in_specs=[pl.BlockSpec(memory_space=pltpu.SMEM)] + [VMEM] * (1 + len(own) + len(sib)),
        out_specs=VMEM,
        compiler_params=PARAMS,
    )(plane, context, *own, *sib)


def add_kernel(core_ref, partial_ref, out_ref):
    quarters, sides, senders, half, width = partial_ref.shape
    middle, part = width // 2, width // 4
    together = width // (part * sides)
    for first in range(0, quarters, together):
        sums = []
        for x in range(first, first + together):
            for s in range(sides):
                total = partial_ref[x, s, 0].astype(jnp.float32)
                for sender in range(1, senders):
                    total += partial_ref[x, s, sender].astype(jnp.float32)
                sums.append(total.astype(jnp.bfloat16))
        for side in range(2):
            core = core_ref[0] if side == 0 else 1 - core_ref[0]
            at = (core * (quarters // together) + first // together) * width
            cols = pl.ds(pl.multiple_of(at, width), width)
            for low in range(2):
                at = low * middle + side * part
                out_ref[low * half : (low + 1) * half, cols] = jnp.concatenate(
                    [one[:, at : at + part] for one in sums], axis=1
                )


def add(core, partial):
    quarters, sides, _, half, width = partial.shape
    return pl.pallas_call(
        add_kernel,
        out_shape=jax.ShapeDtypeStruct((2 * half, sides * quarters * width // 2), jnp.bfloat16),
        in_specs=[pl.BlockSpec(memory_space=pltpu.SMEM), VMEM],
        out_specs=VMEM,
        compiler_params=PARAMS,
    )(core, partial)


def exchange(value, axes):
    shape = value.shape
    value = value.reshape(-1, *shape[len(axes) :])
    value = lax.all_to_all(value, axes, split_axis=0, concat_axis=0, tiled=True)
    return value.reshape(shape)


OFFSETS = (0, -1, 1, -2, 2, -3, 3, 4)


def ring(value, axis, size):
    up = [(i, (i + 1) % size) for i in range(size)]
    down = [(i, (i - 1) % size) for i in range(size)]
    blocks, behind, ahead = [value], value, value
    for _ in range(size // 2 - 1):
        behind = lax.ppermute(behind, axis, up)
        ahead = lax.ppermute(ahead, axis, down)
        blocks += [behind, ahead]
    return blocks + [lax.ppermute(ahead, axis, down)]


def local(
    decoder_query,
    decoder_memory,
    neighbour_query,
    neighbour_key,
    neighbour_value,
    neighbour_table,
    output_weight,
):
    folded = fold(output_weight, 8)
    folded = exchange(folded.reshape(4, 2, *folded.shape[1:]), ("x", "yl"))
    blocks = ring(regroup(folded), "z", 8)

    neighbours = pack(neighbour_query, neighbour_key, neighbour_value, 4, 4)
    neighbours = exchange(neighbours, ("x", "yh"))
    table = neighbour_table & 3
    context = attention(table, decoder_query, decoder_memory, neighbours, blocks[-3:-1])
    context = repeat(context, 8, blocks[-1:])
    own = stack(blocks, context)
    sib = [lax.ppermute(block, "c", [(0, 1), (1, 0)]) for block in own]
    context = exchange(context.reshape(4, 2, *context.shape[1:]), ("x", "yl"))
    plane = lax.axis_index("z").astype(jnp.int32).reshape(1)
    partial = exchange(project(plane, context, own, sib), ("x", "yl", "yh"))
    core = lax.axis_index("c").astype(jnp.int32).reshape(1)
    return add(core, partial)


def solution(mesh):
    inner = Mesh(mesh.devices.reshape(8, 2, 2, 4, 4), AXES)
    return jax.shard_map(
        local,
        mesh=inner,
        in_specs=(
            P(DP, TENSOR),
            P(None, DP, TENSOR),
            P(AXES, None),
            P(AXES, None),
            P(AXES, None),
            P(DP, None),
            P(TENSOR, DP),
        ),
        out_specs=P(DP, TENSOR),
        check_vma=False,
    )
```

```python
import math

import jax
import jax.numpy as jnp
from jax import lax
from jax.experimental import pallas as pl
from jax.experimental.pallas import tpu as pltpu
from jax.sharding import Mesh
from jax.sharding import PartitionSpec as P

HD = 128
STRETCH = 64
NBLEN = 128
SCALE = 1.0 / math.sqrt(HD)

AXES = ("z", "yl", "c", "yh", "x")
DP = ("z", "yl", "c")
TENSOR = ("yh", "x")


def softmax_rows(scores):
    row_top = jnp.max(scores, axis=-1, keepdims=True)
    expo = jnp.exp(scores - row_top)
    return (expo * (1.0 / jnp.sum(expo, axis=-1, keepdims=True))).astype(jnp.bfloat16)


def rows_times_rows(left, right):
    return lax.dot_general(
        left, right, (((1,), (1,)), ((), ())), preferred_element_type=jnp.float32
    )


def attention_kernel(table_ref, query_ref, memory_ref, nbr_ref, *refs):
    out_ref = refs[-1]
    stretches, per_stretch = table_ref.shape
    heads = query_ref.shape[1] // HD
    parts = [
        (u, slice(u * STRETCH, (u + 1) * STRETCH), slice(h * HD, (h + 1) * HD))
        for u in range(stretches)
        for h in range(heads)
    ]
    places = [[table_ref[u, j] for j in range(per_stretch)] for u in range(stretches)]

    def gathered(kind, u, cols):
        return jnp.concatenate(
            [
                nbr_ref[x, place, kind, :, cols]
                for place in places[u]
                for x in range(nbr_ref.shape[0])
            ],
            axis=0,
        )

    enc_scores = [
        rows_times_rows(gathered(0, u, cols), memory_ref[0, rows, cols]) * SCALE
        for u, rows, cols in parts
    ]
    dec_scores = [
        rows_times_rows(query_ref[rows, cols], gathered(1, u, cols)) * SCALE
        for u, rows, cols in parts
    ]
    enc_probs = [softmax_rows(scores) for scores in enc_scores]
    dec_probs = [softmax_rows(scores) for scores in dec_scores]
    encoded = [
        (
            gathered(2, u, cols).astype(jnp.float32)
            + jnp.dot(probs, memory_ref[1, rows, cols], preferred_element_type=jnp.float32)
        ).astype(jnp.bfloat16)
        for probs, (u, rows, cols) in zip(enc_probs, parts)
    ]
    for probs, values, (_, rows, cols) in zip(dec_probs, encoded, parts):
        context = jnp.dot(probs, values, preferred_element_type=jnp.float32)
        out_ref[rows, cols] = context.astype(jnp.bfloat16)


VMEM = pl.BlockSpec(memory_space=pltpu.VMEM)
ANY = pl.BlockSpec(memory_space=pl.ANY)
HBM = pl.BlockSpec(memory_space=pltpu.HBM)
PARAMS = pltpu.CompilerParams(vmem_limit_bytes=16 * 2**20)
WIDE = pltpu.CompilerParams(vmem_limit_bytes=60 * 2**20)


def attention(table, query, memory, neighbours, after):
    return pl.pallas_call(
        attention_kernel,
        out_shape=jax.ShapeDtypeStruct(query.shape, jnp.bfloat16),
        in_specs=[pl.BlockSpec(memory_space=pltpu.SMEM)] + [VMEM] * 3 + [ANY] * len(after),
        out_specs=VMEM,
        compiler_params=PARAMS,
    )(table, query, memory, neighbours, *after)


def repeat_kernel(value_ref, *refs):
    out_ref, sems = refs[-2:]
    copies = [
        pltpu.make_async_copy(value_ref, out_ref.at[i], sems.at[i]) for i in range(out_ref.shape[0])
    ]
    for copy in copies:
        copy.start()
    for copy in copies:
        copy.wait()


def repeat(value, count, after):
    return pl.pallas_call(
        repeat_kernel,
        out_shape=jax.ShapeDtypeStruct((count, *value.shape), value.dtype),
        in_specs=[VMEM] + [ANY] * len(after),
        out_specs=HBM,
        scratch_shapes=[pltpu.SemaphoreType.DMA((count,))],
        compiler_params=PARAMS,
    )(value, *after)


def pack_kernel(query_ref, key_ref, value_ref, out_ref, held, packed, in_sems, out_sems):
    quarters, highs, _, _, span = out_ref.shape
    loads = [
        pltpu.make_async_copy(ref, held.at[kind], in_sems.at[kind])
        for kind, ref in enumerate((query_ref, key_ref, value_ref))
    ]
    stores = [
        pltpu.make_async_copy(
            packed.at[x, :, kind], out_ref.at[x, :, kind], out_sems.at[x, kind]
        )
        for kind in range(len(loads))
        for x in range(quarters)
    ]
    for load in loads:
        load.start()
    for kind, load in enumerate(loads):
        load.wait()
        for x in range(quarters):
            for y in range(highs):
                at = (y * quarters + x) * span
                packed[x, y, kind] = held[kind, :, at : at + span]
            stores[kind * quarters + x].start()
    for store in stores:
        store.wait()


def pack(query, key, value, quarters, highs):
    rows, cols = query.shape
    span = cols // (quarters * highs)
    shape = (quarters, highs, 3, rows, span)
    return pl.pallas_call(
        pack_kernel,
        out_shape=jax.ShapeDtypeStruct(shape, query.dtype),
        in_specs=[HBM] * 3,
        out_specs=HBM,
        scratch_shapes=[
            pltpu.VMEM((3, rows, cols), query.dtype),
            pltpu.VMEM(shape, query.dtype),
            pltpu.SemaphoreType.DMA((3,)),
            pltpu.SemaphoreType.DMA((quarters, 3)),
        ],
        compiler_params=WIDE,
    )(query, key, value)


def fold_kernel(weight_ref, out_ref):
    eighths, quarter, width = out_ref.shape
    part = weight_ref.shape[1] // eighths
    for e in range(eighths):
        cols = slice(e * part, (e + 1) * part)
        out_ref[e] = jnp.concatenate(
            [weight_ref[k * quarter : (k + 1) * quarter, cols] for k in range(width // part)],
            axis=1,
        )


def fold(weight, eighths):
    rows, cols = weight.shape
    part = cols // eighths
    return pl.pallas_call(
        fold_kernel,
        out_shape=jax.ShapeDtypeStruct((eighths, rows * part // HD, HD), weight.dtype),
        in_specs=[VMEM],
        out_specs=VMEM,
        compiler_params=PARAMS,
    )(weight)


def regroup_kernel(folded_ref, out_ref):
    quarters, senders, quarter, width = folded_ref.shape
    part = width // 4
    for x in range(quarters):
        for k in range(2):
            out_ref[x, k * quarter : (k + 1) * quarter] = jnp.concatenate(
                [
                    folded_ref[x, s, :, at * part : (at + 1) * part]
                    for at in (k, 2 + k)
                    for s in range(senders)
                ],
                axis=1,
            )


def regroup(folded):
    quarters, _, quarter, width = folded.shape
    return pl.pallas_call(
        regroup_kernel,
        out_shape=jax.ShapeDtypeStruct((quarters, 2 * quarter, width), folded.dtype),
        in_specs=[VMEM],
        out_specs=VMEM,
        compiler_params=PARAMS,
    )(folded)


TOGETHER = 4


def stack_kernel(*refs):
    count = (len(refs) - 1) * TOGETHER // (TOGETHER + 1)
    for i in range(count):
        refs[count + 1 + i // TOGETHER][i % TOGETHER] = refs[i][...]


def stack(blocks, after):
    shape = jax.ShapeDtypeStruct((TOGETHER, *blocks[0].shape), blocks[0].dtype)
    outs = len(blocks) // TOGETHER
    return pl.pallas_call(
        stack_kernel,
        out_shape=[shape] * outs,
        in_specs=[VMEM] * len(blocks) + [ANY],
        out_specs=[VMEM] * outs,
        compiler_params=PARAMS,
    )(*blocks, after)


def project_kernel(plane_ref, _, context_ref, *refs):
    out_ref = refs[-1]
    stacks = len(refs) // 2
    plane = plane_ref[0]
    quarters, sides, tokens, span = context_ref.shape
    width = refs[0].shape[-1]
    middle, half, part = width // 2, tokens // 2, width // 4
    planes = TOGETHER * stacks
    left = [
        jnp.concatenate([context_ref[x, s] for s in range(sides)], axis=0)
        for x in range(quarters)
    ]

    def rows_of(index, x):
        own = refs[index // TOGETHER][index % TOGETHER, x]
        sib = refs[stacks + index // TOGETHER][index % TOGETHER, x]
        upper = jnp.concatenate([own[:, :middle], sib[:, :middle]], axis=1)
        lower = jnp.concatenate([own[:, middle:], sib[:, middle:]], axis=1)
        return jnp.concatenate([upper, lower], axis=0)

    totals = []
    for pair in range(planes // 2):
        total = None
        for x in range(quarters):
            right = jnp.concatenate([rows_of(2 * pair, x), rows_of(2 * pair + 1, x)], axis=1)
            term = jnp.dot(left[x], right, preferred_element_type=jnp.float32)
            total = term if total is None else total + term
        totals.append(total.astype(jnp.bfloat16))
    for index in range(planes):
        total = totals[index // 2]
        first = index % 2 * width
        target = lax.rem(plane + OFFSETS[index] + planes, planes)
        for s in range(sides):
            upper = total[s * tokens : s * tokens + half]
            lower = total[s * tokens + half : (s + 1) * tokens]
            for piece in range(2):
                own = slice(first + piece * part, first + (piece + 1) * part)
                sib = slice(own.start + middle, own.stop + middle)
                x = 2 * lax.rem(target, 2) + piece
                out_ref[x, s, lax.div(target, 2)] = jnp.concatenate(
                    [upper[:, own], upper[:, sib], lower[:, own], lower[:, sib]], axis=1
                )


def project(plane, core, context, own, sib):
    quarters, sides, tokens, _ = context.shape
    highs = 2 * TOGETHER * len(own) // quarters
    return pl.pallas_call(
        project_kernel,
        out_shape=jax.ShapeDtypeStruct(
            (quarters, sides, highs, tokens // 2, own[0].shape[-1]), jnp.bfloat16
        ),
        in_specs=[pl.BlockSpec(memory_space=pltpu.SMEM)] * 2 + [VMEM] * (1 + len(own) + len(sib)),
        out_specs=VMEM,
        compiler_params=PARAMS,
    )(plane, core, context, *own, *sib)


def add_kernel(core_ref, partial_ref, out_ref):
    quarters, sides, senders, half, width = partial_ref.shape
    middle, part = width // 2, width // 4
    together = width // (part * sides)
    for first in range(0, quarters, together):
        sums = []
        for x in range(first, first + together):
            for s in range(sides):
                total = partial_ref[x, s, 0].astype(jnp.float32)
                for sender in range(1, senders):
                    total += partial_ref[x, s, sender].astype(jnp.float32)
                sums.append(total.astype(jnp.bfloat16))
        for side in range(2):
            core = core_ref[0] if side == 0 else 1 - core_ref[0]
            at = (core * (quarters // together) + first // together) * width
            cols = pl.ds(pl.multiple_of(at, width), width)
            for low in range(2):
                at = low * middle + side * part
                out_ref[low * half : (low + 1) * half, cols] = jnp.concatenate(
                    [one[:, at : at + part] for one in sums], axis=1
                )


def add(core, partial):
    quarters, sides, _, half, width = partial.shape
    return pl.pallas_call(
        add_kernel,
        out_shape=jax.ShapeDtypeStruct((2 * half, sides * quarters * width // 2), jnp.bfloat16),
        in_specs=[pl.BlockSpec(memory_space=pltpu.SMEM), VMEM],
        out_specs=VMEM,
        compiler_params=PARAMS,
    )(core, partial)


def exchange(value, axes):
    shape = value.shape
    value = value.reshape(-1, *shape[len(axes) :])
    value = lax.all_to_all(value, axes, split_axis=0, concat_axis=0, tiled=True)
    return value.reshape(shape)


OFFSETS = (0, -1, 1, -2, 2, -3, 3, 4)


def ring(value, axis, size):
    up = [(i, (i + 1) % size) for i in range(size)]
    down = [(i, (i - 1) % size) for i in range(size)]
    blocks, behind, ahead = [value], value, value
    for _ in range(size // 2 - 1):
        behind = lax.ppermute(behind, axis, up)
        ahead = lax.ppermute(ahead, axis, down)
        blocks += [behind, ahead]
    return blocks + [lax.ppermute(ahead, axis, down)]


def local(
    decoder_query,
    decoder_memory,
    neighbour_query,
    neighbour_key,
    neighbour_value,
    neighbour_table,
    output_weight,
):
    folded = fold(output_weight, 8)
    folded = exchange(folded.reshape(4, 2, *folded.shape[1:]), ("x", "yl"))
    blocks = ring(regroup(folded), "z", 8)

    neighbours = pack(neighbour_query, neighbour_key, neighbour_value, 4, 4)
    neighbours = exchange(neighbours, ("x", "yh"))
    table = neighbour_table & 3
    context = attention(table, decoder_query, decoder_memory, neighbours, blocks[-3:-1])
    context = repeat(context, 8, blocks[-1:])
    own = stack(blocks, context)
    sib = [lax.ppermute(block, "c", [(0, 1), (1, 0)]) for block in own]
    context = exchange(context.reshape(4, 2, *context.shape[1:]), ("x", "yl"))
    plane = lax.axis_index("z").astype(jnp.int32).reshape(1)
    core = lax.axis_index("c").astype(jnp.int32).reshape(1)
    partial = exchange(project(plane, core, context, own, sib), ("x", "yl", "yh"))
    return add(core, partial)


def solution(mesh):
    inner = Mesh(mesh.devices.reshape(8, 2, 2, 4, 4), AXES)
    return jax.shard_map(
        local,
        mesh=inner,
        in_specs=(
            P(DP, TENSOR),
            P(None, DP, TENSOR),
            P(AXES, None),
            P(AXES, None),
            P(AXES, None),
            P(DP, None),
            P(TENSOR, DP),
        ),
        out_specs=P(DP, TENSOR),
        check_vma=False,
    )
```

```python
import math

import jax
import jax.numpy as jnp
from jax import lax
from jax.experimental import pallas as pl
from jax.experimental.pallas import tpu as pltpu
from jax.sharding import Mesh
from jax.sharding import PartitionSpec as P

HD = 128
STRETCH = 64
NBLEN = 128
SCALE = 1.0 / math.sqrt(HD)

AXES = ("z", "yl", "c", "yh", "x")
DP = ("z", "yl", "c")
TENSOR = ("yh", "x")


def softmax_rows(scores):
    row_top = jnp.max(scores, axis=-1, keepdims=True)
    expo = jnp.exp(scores - row_top)
    return (expo * (1.0 / jnp.sum(expo, axis=-1, keepdims=True))).astype(jnp.bfloat16)


def rows_times_rows(left, right):
    return lax.dot_general(
        left, right, (((1,), (1,)), ((), ())), preferred_element_type=jnp.float32
    )


def attention_kernel(table_ref, query_ref, memory_ref, nbr_ref, *refs):
    out_ref = refs[-1]
    stretches, per_stretch = table_ref.shape
    heads = query_ref.shape[1] // HD
    parts = [
        (u, slice(u * STRETCH, (u + 1) * STRETCH), slice(h * HD, (h + 1) * HD))
        for u in range(stretches)
        for h in range(heads)
    ]
    places = [[table_ref[u, j] for j in range(per_stretch)] for u in range(stretches)]

    def gathered(kind, u, cols):
        return jnp.concatenate(
            [
                nbr_ref[x, place, kind, :, cols]
                for place in places[u]
                for x in range(nbr_ref.shape[0])
            ],
            axis=0,
        )

    enc_scores = [
        rows_times_rows(gathered(0, u, cols), memory_ref[0, rows, cols]) * SCALE
        for u, rows, cols in parts
    ]
    dec_scores = [
        rows_times_rows(query_ref[rows, cols], gathered(1, u, cols)) * SCALE
        for u, rows, cols in parts
    ]
    enc_probs = [softmax_rows(scores) for scores in enc_scores]
    dec_probs = [softmax_rows(scores) for scores in dec_scores]
    encoded = [
        (
            gathered(2, u, cols).astype(jnp.float32)
            + jnp.dot(probs, memory_ref[1, rows, cols], preferred_element_type=jnp.float32)
        ).astype(jnp.bfloat16)
        for probs, (u, rows, cols) in zip(enc_probs, parts)
    ]
    for probs, values, (_, rows, cols) in zip(dec_probs, encoded, parts):
        context = jnp.dot(probs, values, preferred_element_type=jnp.float32)
        out_ref[rows, cols] = context.astype(jnp.bfloat16)


VMEM = pl.BlockSpec(memory_space=pltpu.VMEM)
ANY = pl.BlockSpec(memory_space=pl.ANY)
HBM = pl.BlockSpec(memory_space=pltpu.HBM)
PARAMS = pltpu.CompilerParams(vmem_limit_bytes=16 * 2**20)
WIDE = pltpu.CompilerParams(vmem_limit_bytes=60 * 2**20)


def attention(table, query, memory, neighbours, after):
    return pl.pallas_call(
        attention_kernel,
        out_shape=jax.ShapeDtypeStruct(query.shape, jnp.bfloat16),
        in_specs=[pl.BlockSpec(memory_space=pltpu.SMEM)] + [VMEM] * 3 + [ANY] * len(after),
        out_specs=VMEM,
        compiler_params=PARAMS,
    )(table, query, memory, neighbours, *after)


def repeat_kernel(value_ref, *refs):
    out_ref, sems = refs[-2:]
    copies = [
        pltpu.make_async_copy(value_ref, out_ref.at[i], sems.at[i]) for i in range(out_ref.shape[0])
    ]
    for copy in copies:
        copy.start()
    for copy in copies:
        copy.wait()


def repeat(value, count, after):
    return pl.pallas_call(
        repeat_kernel,
        out_shape=jax.ShapeDtypeStruct((count, *value.shape), value.dtype),
        in_specs=[VMEM] + [ANY] * len(after),
        out_specs=HBM,
        scratch_shapes=[pltpu.SemaphoreType.DMA((count,))],
        compiler_params=PARAMS,
    )(value, *after)


def pack_kernel(query_ref, key_ref, value_ref, out_ref, held, packed, in_sems, out_sems):
    quarters, highs, _, _, span = out_ref.shape
    loads = [
        pltpu.make_async_copy(ref, held.at[kind], in_sems.at[kind])
        for kind, ref in enumerate((query_ref, key_ref, value_ref))
    ]
    stores = [
        pltpu.make_async_copy(
            packed.at[x, :, kind], out_ref.at[x, :, kind], out_sems.at[x, kind]
        )
        for kind in range(len(loads))
        for x in range(quarters)
    ]
    for load in loads:
        load.start()
    for kind, load in enumerate(loads):
        load.wait()
        for x in range(quarters):
            for y in range(highs):
                at = (y * quarters + x) * span
                packed[x, y, kind] = held[kind, :, at : at + span]
            stores[kind * quarters + x].start()
    for store in stores:
        store.wait()


def pack(query, key, value, quarters, highs):
    rows, cols = query.shape
    span = cols // (quarters * highs)
    shape = (quarters, highs, 3, rows, span)
    return pl.pallas_call(
        pack_kernel,
        out_shape=jax.ShapeDtypeStruct(shape, query.dtype),
        in_specs=[HBM] * 3,
        out_specs=HBM,
        scratch_shapes=[
            pltpu.VMEM((3, rows, cols), query.dtype),
            pltpu.VMEM(shape, query.dtype),
            pltpu.SemaphoreType.DMA((3,)),
            pltpu.SemaphoreType.DMA((quarters, 3)),
        ],
        compiler_params=WIDE,
    )(query, key, value)


def fold_kernel(weight_ref, out_ref):
    eighths, quarter, width = out_ref.shape
    part = weight_ref.shape[1] // eighths
    for e in range(eighths):
        cols = slice(e * part, (e + 1) * part)
        out_ref[e] = jnp.concatenate(
            [weight_ref[k * quarter : (k + 1) * quarter, cols] for k in range(width // part)],
            axis=1,
        )


def fold(weight, eighths):
    rows, cols = weight.shape
    part = cols // eighths
    return pl.pallas_call(
        fold_kernel,
        out_shape=jax.ShapeDtypeStruct((eighths, rows * part // HD, HD), weight.dtype),
        in_specs=[VMEM],
        out_specs=VMEM,
        compiler_params=PARAMS,
    )(weight)


def regroup_kernel(folded_ref, out_ref):
    quarters, senders, quarter, width = folded_ref.shape
    part = width // 4
    for x in range(quarters):
        for k in range(2):
            out_ref[x, k * quarter : (k + 1) * quarter] = jnp.concatenate(
                [
                    folded_ref[x, s, :, at * part : (at + 1) * part]
                    for at in (k, 2 + k)
                    for s in range(senders)
                ],
                axis=1,
            )


def regroup(folded):
    quarters, _, quarter, width = folded.shape
    return pl.pallas_call(
        regroup_kernel,
        out_shape=jax.ShapeDtypeStruct((quarters, 2 * quarter, width), folded.dtype),
        in_specs=[VMEM],
        out_specs=VMEM,
        compiler_params=PARAMS,
    )(folded)


TOGETHER = 4


def stack_kernel(*refs):
    count = (len(refs) - 1) * TOGETHER // (TOGETHER + 1)
    for i in range(count):
        refs[count + 1 + i // TOGETHER][i % TOGETHER] = refs[i][...]


def stack(blocks, after):
    shape = jax.ShapeDtypeStruct((TOGETHER, *blocks[0].shape), blocks[0].dtype)
    outs = len(blocks) // TOGETHER
    return pl.pallas_call(
        stack_kernel,
        out_shape=[shape] * outs,
        in_specs=[VMEM] * len(blocks) + [ANY],
        out_specs=[VMEM] * outs,
        compiler_params=PARAMS,
    )(*blocks, after)


def project_kernel(plane_ref, _, context_ref, *refs):
    out_ref = refs[-1]
    stacks = len(refs) // 2
    plane = plane_ref[0]
    quarters, sides, tokens, span = context_ref.shape
    width = refs[0].shape[-1]
    middle, half, part = width // 2, tokens // 2, width // 4
    planes = TOGETHER * stacks
    left = jnp.concatenate(
        [
            jnp.concatenate([context_ref[x, s] for s in range(sides)], axis=0)
            for x in range(quarters)
        ],
        axis=1,
    )

    def rows_of(index, x):
        own = refs[index // TOGETHER][index % TOGETHER, x]
        sib = refs[stacks + index // TOGETHER][index % TOGETHER, x]
        upper = jnp.concatenate([own[:, :middle], sib[:, :middle]], axis=1)
        lower = jnp.concatenate([own[:, middle:], sib[:, middle:]], axis=1)
        return jnp.concatenate([upper, lower], axis=0)

    totals = []
    for pair in range(planes // 2):
        right = jnp.concatenate(
            [
                jnp.concatenate([rows_of(2 * pair, x), rows_of(2 * pair + 1, x)], axis=1)
                for x in range(quarters)
            ],
            axis=0,
        )
        total = jnp.dot(left, right, preferred_element_type=jnp.float32)
        totals.append(total.astype(jnp.bfloat16))
    for index in range(planes):
        total = totals[index // 2]
        first = index % 2 * width
        target = lax.rem(plane + OFFSETS[index] + planes, planes)
        for s in range(sides):
            upper = total[s * tokens : s * tokens + half]
            lower = total[s * tokens + half : (s + 1) * tokens]
            for piece in range(2):
                own = slice(first + piece * part, first + (piece + 1) * part)
                sib = slice(own.start + middle, own.stop + middle)
                x = 2 * lax.rem(target, 2) + piece
                out_ref[x, s, lax.div(target, 2)] = jnp.concatenate(
                    [upper[:, own], upper[:, sib], lower[:, own], lower[:, sib]], axis=1
                )


def project(plane, core, context, own, sib):
    quarters, sides, tokens, _ = context.shape
    highs = 2 * TOGETHER * len(own) // quarters
    return pl.pallas_call(
        project_kernel,
        out_shape=jax.ShapeDtypeStruct(
            (quarters, sides, highs, tokens // 2, own[0].shape[-1]), jnp.bfloat16
        ),
        in_specs=[pl.BlockSpec(memory_space=pltpu.SMEM)] * 2 + [VMEM] * (1 + len(own) + len(sib)),
        out_specs=VMEM,
        compiler_params=PARAMS,
    )(plane, core, context, *own, *sib)


def add_kernel(core_ref, partial_ref, out_ref):
    quarters, sides, senders, half, width = partial_ref.shape
    middle, part = width // 2, width // 4
    together = width // (part * sides)
    for first in range(0, quarters, together):
        sums = []
        for x in range(first, first + together):
            for s in range(sides):
                total = partial_ref[x, s, 0].astype(jnp.float32)
                for sender in range(1, senders):
                    total += partial_ref[x, s, sender].astype(jnp.float32)
                sums.append(total.astype(jnp.bfloat16))
        for side in range(2):
            core = core_ref[0] if side == 0 else 1 - core_ref[0]
            at = (core * (quarters // together) + first // together) * width
            cols = pl.ds(pl.multiple_of(at, width), width)
            for low in range(2):
                at = low * middle + side * part
                out_ref[low * half : (low + 1) * half, cols] = jnp.concatenate(
                    [one[:, at : at + part] for one in sums], axis=1
                )


def add(core, partial):
    quarters, sides, _, half, width = partial.shape
    return pl.pallas_call(
        add_kernel,
        out_shape=jax.ShapeDtypeStruct((2 * half, sides * quarters * width // 2), jnp.bfloat16),
        in_specs=[pl.BlockSpec(memory_space=pltpu.SMEM), VMEM],
        out_specs=VMEM,
        compiler_params=PARAMS,
    )(core, partial)


def exchange(value, axes):
    shape = value.shape
    value = value.reshape(-1, *shape[len(axes) :])
    value = lax.all_to_all(value, axes, split_axis=0, concat_axis=0, tiled=True)
    return value.reshape(shape)


OFFSETS = (0, -1, 1, -2, 2, -3, 3, 4)


def ring(value, axis, size):
    up = [(i, (i + 1) % size) for i in range(size)]
    down = [(i, (i - 1) % size) for i in range(size)]
    blocks, behind, ahead = [value], value, value
    for _ in range(size // 2 - 1):
        behind = lax.ppermute(behind, axis, up)
        ahead = lax.ppermute(ahead, axis, down)
        blocks += [behind, ahead]
    return blocks + [lax.ppermute(ahead, axis, down)]


def local(
    decoder_query,
    decoder_memory,
    neighbour_query,
    neighbour_key,
    neighbour_value,
    neighbour_table,
    output_weight,
):
    folded = fold(output_weight, 8)
    folded = exchange(folded.reshape(4, 2, *folded.shape[1:]), ("x", "yl"))
    blocks = ring(regroup(folded), "z", 8)

    neighbours = pack(neighbour_query, neighbour_key, neighbour_value, 4, 4)
    neighbours = exchange(neighbours, ("x", "yh"))
    table = neighbour_table & 3
    context = attention(table, decoder_query, decoder_memory, neighbours, blocks[-3:-1])
    context = repeat(context, 8, blocks[-1:])
    own = stack(blocks, context)
    sib = [lax.ppermute(block, "c", [(0, 1), (1, 0)]) for block in own]
    context = exchange(context.reshape(4, 2, *context.shape[1:]), ("x", "yl"))
    plane = lax.axis_index("z").astype(jnp.int32).reshape(1)
    core = lax.axis_index("c").astype(jnp.int32).reshape(1)
    partial = exchange(project(plane, core, context, own, sib), ("x", "yl", "yh"))
    return add(core, partial)


def solution(mesh):
    inner = Mesh(mesh.devices.reshape(8, 2, 2, 4, 4), AXES)
    return jax.shard_map(
        local,
        mesh=inner,
        in_specs=(
            P(DP, TENSOR),
            P(None, DP, TENSOR),
            P(AXES, None),
            P(AXES, None),
            P(AXES, None),
            P(DP, None),
            P(TENSOR, DP),
        ),
        out_specs=P(DP, TENSOR),
        check_vma=False,
    )
```

```python
import math

import jax
import jax.numpy as jnp
from jax import lax
from jax.experimental import pallas as pl
from jax.experimental.pallas import tpu as pltpu
from jax.sharding import Mesh
from jax.sharding import PartitionSpec as P

HD = 128
STRETCH = 64
NBLEN = 128
SCALE = 1.0 / math.sqrt(HD)

AXES = ("z", "yl", "c", "yh", "x")
DP = ("z", "yl", "c")
TENSOR = ("yh", "x")


def softmax_rows(scores):
    row_top = jnp.max(scores, axis=-1, keepdims=True)
    expo = jnp.exp((scores - row_top) * SCALE)
    return (expo * (1.0 / jnp.sum(expo, axis=-1, keepdims=True))).astype(jnp.bfloat16)


def rows_times_rows(left, right):
    return lax.dot_general(
        left, right, (((1,), (1,)), ((), ())), preferred_element_type=jnp.float32
    )


def attention_kernel(table_ref, query_ref, memory_ref, nbr_ref, *refs):
    out_ref = refs[-1]
    stretches, per_stretch = table_ref.shape
    heads = query_ref.shape[1] // HD
    parts = [
        (u, slice(u * STRETCH, (u + 1) * STRETCH), slice(h * HD, (h + 1) * HD))
        for u in range(stretches)
        for h in range(heads)
    ]
    places = [[table_ref[u, j] for j in range(per_stretch)] for u in range(stretches)]

    def gathered(kind, u, cols):
        return jnp.concatenate(
            [
                nbr_ref[x, place, kind, :, cols]
                for place in places[u]
                for x in range(nbr_ref.shape[0])
            ],
            axis=0,
        )

    enc_scores = [
        rows_times_rows(gathered(0, u, cols), memory_ref[0, rows, cols])
        for u, rows, cols in parts
    ]
    dec_scores = [
        rows_times_rows(query_ref[rows, cols], gathered(1, u, cols))
        for u, rows, cols in parts
    ]
    enc_probs = [softmax_rows(scores) for scores in enc_scores]
    dec_probs = [softmax_rows(scores) for scores in dec_scores]
    encoded = [
        (
            gathered(2, u, cols).astype(jnp.float32)
            + jnp.dot(probs, memory_ref[1, rows, cols], preferred_element_type=jnp.float32)
        ).astype(jnp.bfloat16)
        for probs, (u, rows, cols) in zip(enc_probs, parts)
    ]
    for probs, values, (_, rows, cols) in zip(dec_probs, encoded, parts):
        context = jnp.dot(probs, values, preferred_element_type=jnp.float32)
        out_ref[rows, cols] = context.astype(jnp.bfloat16)


VMEM = pl.BlockSpec(memory_space=pltpu.VMEM)
ANY = pl.BlockSpec(memory_space=pl.ANY)
HBM = pl.BlockSpec(memory_space=pltpu.HBM)
PARAMS = pltpu.CompilerParams(vmem_limit_bytes=16 * 2**20)
WIDE = pltpu.CompilerParams(vmem_limit_bytes=60 * 2**20)


def attention(table, query, memory, neighbours, after):
    return pl.pallas_call(
        attention_kernel,
        out_shape=jax.ShapeDtypeStruct(query.shape, jnp.bfloat16),
        in_specs=[pl.BlockSpec(memory_space=pltpu.SMEM)] + [VMEM] * 3 + [ANY] * len(after),
        out_specs=VMEM,
        compiler_params=PARAMS,
    )(table, query, memory, neighbours, *after)


def repeat_kernel(value_ref, *refs):
    out_ref, sems = refs[-2:]
    copies = [
        pltpu.make_async_copy(value_ref, out_ref.at[i], sems.at[i]) for i in range(out_ref.shape[0])
    ]
    for copy in copies:
        copy.start()
    for copy in copies:
        copy.wait()


def repeat(value, count, after):
    return pl.pallas_call(
        repeat_kernel,
        out_shape=jax.ShapeDtypeStruct((count, *value.shape), value.dtype),
        in_specs=[VMEM] + [ANY] * len(after),
        out_specs=HBM,
        scratch_shapes=[pltpu.SemaphoreType.DMA((count,))],
        compiler_params=PARAMS,
    )(value, *after)


def pack_kernel(query_ref, key_ref, value_ref, out_ref, held, packed, in_sems, out_sems):
    quarters, highs, _, _, span = out_ref.shape
    loads = [
        pltpu.make_async_copy(ref, held.at[kind], in_sems.at[kind])
        for kind, ref in enumerate((query_ref, key_ref, value_ref))
    ]
    stores = [
        pltpu.make_async_copy(
            packed.at[x, :, kind], out_ref.at[x, :, kind], out_sems.at[x, kind]
        )
        for kind in range(len(loads))
        for x in range(quarters)
    ]
    for load in loads:
        load.start()
    for kind, load in enumerate(loads):
        load.wait()
        for x in range(quarters):
            for y in range(highs):
                at = (y * quarters + x) * span
                packed[x, y, kind] = held[kind, :, at : at + span]
            stores[kind * quarters + x].start()
    for store in stores:
        store.wait()


def pack(query, key, value, quarters, highs):
    rows, cols = query.shape
    span = cols // (quarters * highs)
    shape = (quarters, highs, 3, rows, span)
    return pl.pallas_call(
        pack_kernel,
        out_shape=jax.ShapeDtypeStruct(shape, query.dtype),
        in_specs=[HBM] * 3,
        out_specs=HBM,
        scratch_shapes=[
            pltpu.VMEM((3, rows, cols), query.dtype),
            pltpu.VMEM(shape, query.dtype),
            pltpu.SemaphoreType.DMA((3,)),
            pltpu.SemaphoreType.DMA((quarters, 3)),
        ],
        compiler_params=WIDE,
    )(query, key, value)


def fold_kernel(weight_ref, out_ref):
    eighths, quarter, width = out_ref.shape
    part = weight_ref.shape[1] // eighths
    for e in range(eighths):
        cols = slice(e * part, (e + 1) * part)
        out_ref[e] = jnp.concatenate(
            [weight_ref[k * quarter : (k + 1) * quarter, cols] for k in range(width // part)],
            axis=1,
        )


def fold(weight, eighths):
    rows, cols = weight.shape
    part = cols // eighths
    return pl.pallas_call(
        fold_kernel,
        out_shape=jax.ShapeDtypeStruct((eighths, rows * part // HD, HD), weight.dtype),
        in_specs=[VMEM],
        out_specs=VMEM,
        compiler_params=PARAMS,
    )(weight)


def regroup_kernel(folded_ref, out_ref):
    quarters, senders, quarter, width = folded_ref.shape
    part = width // 4
    for x in range(quarters):
        for k in range(2):
            out_ref[x, k * quarter : (k + 1) * quarter] = jnp.concatenate(
                [
                    folded_ref[x, s, :, at * part : (at + 1) * part]
                    for at in (k, 2 + k)
                    for s in range(senders)
                ],
                axis=1,
            )


def regroup(folded):
    quarters, _, quarter, width = folded.shape
    return pl.pallas_call(
        regroup_kernel,
        out_shape=jax.ShapeDtypeStruct((quarters, 2 * quarter, width), folded.dtype),
        in_specs=[VMEM],
        out_specs=VMEM,
        compiler_params=PARAMS,
    )(folded)


TOGETHER = 4


def stack_kernel(*refs):
    count = (len(refs) - 1) * TOGETHER // (TOGETHER + 1)
    for i in range(count):
        refs[count + 1 + i // TOGETHER][i % TOGETHER] = refs[i][...]


def stack(blocks, after):
    shape = jax.ShapeDtypeStruct((TOGETHER, *blocks[0].shape), blocks[0].dtype)
    outs = len(blocks) // TOGETHER
    return pl.pallas_call(
        stack_kernel,
        out_shape=[shape] * outs,
        in_specs=[VMEM] * len(blocks) + [ANY],
        out_specs=[VMEM] * outs,
        compiler_params=PARAMS,
    )(*blocks, after)


def project_kernel(plane_ref, _, context_ref, *refs):
    out_ref = refs[-1]
    stacks = len(refs) // 2
    plane = plane_ref[0]
    quarters, sides, tokens, span = context_ref.shape
    width = refs[0].shape[-1]
    middle, half, part = width // 2, tokens // 2, width // 4
    planes = TOGETHER * stacks
    left = jnp.concatenate(
        [
            jnp.concatenate([context_ref[x, s] for s in range(sides)], axis=0)
            for x in range(quarters)
        ],
        axis=1,
    )

    def rows_of(index, x):
        own = refs[index // TOGETHER][index % TOGETHER, x]
        sib = refs[stacks + index // TOGETHER][index % TOGETHER, x]
        upper = jnp.concatenate([own[:, :middle], sib[:, :middle]], axis=1)
        lower = jnp.concatenate([own[:, middle:], sib[:, middle:]], axis=1)
        return jnp.concatenate([upper, lower], axis=0)

    totals = []
    for pair in range(planes // 2):
        right = jnp.concatenate(
            [
                jnp.concatenate([rows_of(2 * pair, x), rows_of(2 * pair + 1, x)], axis=1)
                for x in range(quarters)
            ],
            axis=0,
        )
        total = jnp.dot(left, right, preferred_element_type=jnp.float32)
        totals.append(total.astype(jnp.bfloat16))
    for index in range(planes):
        total = totals[index // 2]
        first = index % 2 * width
        target = lax.rem(plane + OFFSETS[index] + planes, planes)
        for s in range(sides):
            upper = total[s * tokens : s * tokens + half]
            lower = total[s * tokens + half : (s + 1) * tokens]
            for piece in range(2):
                own = slice(first + piece * part, first + (piece + 1) * part)
                sib = slice(own.start + middle, own.stop + middle)
                x = 2 * lax.rem(target, 2) + piece
                out_ref[x, s, lax.div(target, 2)] = jnp.concatenate(
                    [upper[:, own], upper[:, sib], lower[:, own], lower[:, sib]], axis=1
                )


def project(plane, core, context, own, sib):
    quarters, sides, tokens, _ = context.shape
    highs = 2 * TOGETHER * len(own) // quarters
    return pl.pallas_call(
        project_kernel,
        out_shape=jax.ShapeDtypeStruct(
            (quarters, sides, highs, tokens // 2, own[0].shape[-1]), jnp.bfloat16
        ),
        in_specs=[pl.BlockSpec(memory_space=pltpu.SMEM)] * 2 + [VMEM] * (1 + len(own) + len(sib)),
        out_specs=VMEM,
        compiler_params=PARAMS,
    )(plane, core, context, *own, *sib)


def add_kernel(core_ref, partial_ref, out_ref):
    quarters, sides, senders, half, width = partial_ref.shape
    middle, part = width // 2, width // 4
    together = width // (part * sides)
    for first in range(0, quarters, together):
        sums = []
        for x in range(first, first + together):
            for s in range(sides):
                total = partial_ref[x, s, 0].astype(jnp.float32)
                for sender in range(1, senders):
                    total += partial_ref[x, s, sender].astype(jnp.float32)
                sums.append(total.astype(jnp.bfloat16))
        for side in range(2):
            core = core_ref[0] if side == 0 else 1 - core_ref[0]
            at = (core * (quarters // together) + first // together) * width
            cols = pl.ds(pl.multiple_of(at, width), width)
            for low in range(2):
                at = low * middle + side * part
                out_ref[low * half : (low + 1) * half, cols] = jnp.concatenate(
                    [one[:, at : at + part] for one in sums], axis=1
                )


def add(core, partial):
    quarters, sides, _, half, width = partial.shape
    return pl.pallas_call(
        add_kernel,
        out_shape=jax.ShapeDtypeStruct((2 * half, sides * quarters * width // 2), jnp.bfloat16),
        in_specs=[pl.BlockSpec(memory_space=pltpu.SMEM), VMEM],
        out_specs=VMEM,
        compiler_params=PARAMS,
    )(core, partial)


def exchange(value, axes):
    shape = value.shape
    value = value.reshape(-1, *shape[len(axes) :])
    value = lax.all_to_all(value, axes, split_axis=0, concat_axis=0, tiled=True)
    return value.reshape(shape)


OFFSETS = (0, -1, 1, -2, 2, -3, 3, 4)


def ring(value, axis, size):
    up = [(i, (i + 1) % size) for i in range(size)]
    down = [(i, (i - 1) % size) for i in range(size)]
    blocks, behind, ahead = [value], value, value
    for _ in range(size // 2 - 1):
        behind = lax.ppermute(behind, axis, up)
        ahead = lax.ppermute(ahead, axis, down)
        blocks += [behind, ahead]
    return blocks + [lax.ppermute(ahead, axis, down)]


def local(
    decoder_query,
    decoder_memory,
    neighbour_query,
    neighbour_key,
    neighbour_value,
    neighbour_table,
    output_weight,
):
    folded = fold(output_weight, 8)
    folded = exchange(folded.reshape(4, 2, *folded.shape[1:]), ("x", "yl"))
    blocks = ring(regroup(folded), "z", 8)

    neighbours = pack(neighbour_query, neighbour_key, neighbour_value, 4, 4)
    neighbours = exchange(neighbours, ("x", "yh"))
    table = neighbour_table & 3
    context = attention(table, decoder_query, decoder_memory, neighbours, blocks[-3:-1])
    context = repeat(context, 8, blocks[-1:])
    own = stack(blocks, context)
    sib = [lax.ppermute(block, "c", [(0, 1), (1, 0)]) for block in own]
    context = exchange(context.reshape(4, 2, *context.shape[1:]), ("x", "yl"))
    plane = lax.axis_index("z").astype(jnp.int32).reshape(1)
    core = lax.axis_index("c").astype(jnp.int32).reshape(1)
    partial = exchange(project(plane, core, context, own, sib), ("x", "yl", "yh"))
    return add(core, partial)


def solution(mesh):
    inner = Mesh(mesh.devices.reshape(8, 2, 2, 4, 4), AXES)
    return jax.shard_map(
        local,
        mesh=inner,
        in_specs=(
            P(DP, TENSOR),
            P(None, DP, TENSOR),
            P(AXES, None),
            P(AXES, None),
            P(AXES, None),
            P(DP, None),
            P(TENSOR, DP),
        ),
        out_specs=P(DP, TENSOR),
        check_vma=False,
    )
```
